256 devices in a mesh: lon: 8 (over x, core), lat: 8 (over z), mem: 4 (over y).
Axes of the slice: x: 4, y: 4, z: 8, core: 2. Of those that a mesh axis runs over, the one named last changes fastest.
Arguments:
- control: float32 [640, 64, 1024], P('mem', 'lat', 'lon'), may hold values from -6 to 6
- residual: float32 [640, 64, 1024], P('mem', 'lat', 'lon'), may hold values from -6 to 6
- direction: float32 [640, 64, 1024], P('mem', 'lat', 'lon'), may hold values from -6 to 6
- members: bfloat16 [80, 32, 64, 1024], P('mem', None, 'lat', 'lon'), may hold values from -0.625 to 0.625
- vert_modes: float32 [8, 32], replicated, may hold values from -2 to 2
- eig_count: int32 [80], P('mem'), may hold values from 1 to 8, as said below
- lon_decay: float32 [64], P('lat'), may hold values from 0.00048828125 to 0.03125
- lat_decay: float32 [1024], P('lon'), may hold values from 0.0078125 to 0.5
- obs_weight: float32 [32, 64, 1024], P(None, 'lat', 'lon'), may hold values from 0.25 to 4
Outputs:
- new_control: float32 [640, 64, 1024], P('mem', 'lat', 'lon')
- new_residual: float32 [640, 64, 1024], P('mem', 'lat', 'lon')
- new_direction: float32 [640, 64, 1024], P('mem', 'lat', 'lon')
The draws below stay inside these ranges and needn't reach their ends.
Inputs may be any that keep to these rules, and one draw needn't show every extreme that they name: Member m uses its first eig_count[m] vertical modes; some member uses all 8.
All inputs are finite; a program needn't handle non-finite values.
Results may differ from the reference program's by a relative error of at most 0.0009.
Values sent between devices are 32-bit elements; how exact they have to be, the bound alone decides.
A program may use at most 64 MiB of HBM per device.

```python
import math
import jax
import jax.numpy as jnp
from jax import lax

LEV = 32
E = 8
MEMBERS = 80
KMOD = 640
NLON = 1024
NLAT = 64


def draw_eig_count(key, part):
    counts = jax.random.randint(jax.random.fold_in(key, 11), (MEMBERS,), 1, E + 1)
    chosen = jax.random.randint(jax.random.fold_in(key, 12), (), 0, MEMBERS)
    return jnp.where(jnp.arange(MEMBERS) == chosen, E, counts).astype(jnp.int32)


def steps_of(own_key, shape, cuts, least, high):
    gain = 1.0
    for dim, shards_of in cuts:
        heights = jax.random.uniform(jax.random.fold_in(jax.random.fold_in(own_key, 6), dim), (shards_of,), jnp.float32, least / len(cuts), high / len(cuts))
        gain = gain * jnp.repeat(jnp.exp(heights), shape[dim] // shards_of).reshape((-1,) + (1,) * (len(shape) - 1 - dim))
    return gain


def normal_values(own_key, shape, scale, reach, split=(), kind=jnp.bfloat16):
    array = scale * jax.random.normal(own_key, shape, jnp.float32)
    if split:
        array = array * steps_of(own_key, shape, split, -0.22, 0.18)
    return jnp.clip(array, -reach, reach).astype(kind)


def setup_inputs(seed: int = 0) -> dict:
    splits = jax.random.split(jax.random.key(seed), 10)
    return {
        "control": normal_values(splits[0], (KMOD, NLAT, NLON), 1.0, 6.0, ((0, 4), (1, 8), (2, 8)), jnp.float32),
        "residual": normal_values(splits[1], (KMOD, NLAT, NLON), 1.0, 6.0, ((0, 4), (1, 8), (2, 8)), jnp.float32),
        "direction": normal_values(splits[2], (KMOD, NLAT, NLON), 1.0, 6.0, ((0, 4), (1, 8), (2, 8)), jnp.float32),
        "members": normal_values(splits[3], (MEMBERS, LEV, NLAT, NLON), (1.0 / MEMBERS ** 0.5), 0.625, ((0, 4), (2, 8), (3, 8))),
        "vert_modes": normal_values(splits[4], (E, LEV), (1.0 / E ** 0.5), 2.0, (), jnp.float32),
        "eig_count": draw_eig_count(jax.random.fold_in(splits[9], 71), 0),
        "lon_decay": jnp.clip(jnp.exp(math.log(0.03125) - 4.158883 * jax.random.uniform(splits[6], (NLAT,), jnp.float32) ** steps_of(splits[6], (NLAT,), ((0, 8),), -0.2, 0.2)), 0.00048828125, 0.03125),
        "lat_decay": jnp.clip(jnp.exp(math.log(0.5) - 4.158883 * jax.random.uniform(splits[7], (NLON,), jnp.float32) ** steps_of(splits[7], (NLON,), ((0, 8),), -0.2, 0.2)), 0.0078125, 0.5),
        "obs_weight": jnp.clip(jnp.exp(math.log(4.0) - 2.7725887 * jax.random.uniform(splits[8], (LEV, NLAT, NLON), jnp.float32) ** steps_of(splits[8], (LEV, NLAT, NLON), ((1, 8), (2, 8)), -0.2, 0.2)), 0.25, 4.0),
    }


highest = lax.Precision.HIGHEST

def binomial(offset, degree):
    result = jnp.ones_like(offset)
    for factor in range(degree):
        result = result * (offset + factor + 1.0) / (factor + 1.0)
    return result

def transition(decays, length):
    leakage = 1.0 - jnp.exp(-decays)
    closing = jnp.exp(-length * decays)
    zeroes = jnp.zeros_like(decays)
    matrix_rows = []
    for target in range(4):
        entries = []
        for source in range(4):
            if source <= target:
                spread = target - source
                entries.append(binomial(jnp.full_like(decays, length - 1.0), spread) * leakage ** spread * closing)
            else:
                entries.append(zeroes)
        matrix_rows.append(jnp.stack(entries))
    return jnp.stack(matrix_rows)

def periodic_start(matrix, totals):
    solved = []
    for target in range(4):
        running = totals[target]
        for source in range(target):
            running = running + matrix[target, source] * solved[source]
        solved.append(running / (1.0 - matrix[target, target]))
    return jnp.stack(solved)

def filter_last(fields, decays, periodic, backward):
    retain = jnp.exp(-decays)
    leakage = 1.0 - retain
    scaled = fields * (2.5 / jnp.sqrt(leakage))[:, None]
    if backward:
        scaled = scaled[:, :, ::-1]
    inputs = jnp.moveaxis(scaled, 2, 0)

    def advance(states, column):
        section_one = retain * states[0] + leakage * column
        section_two = retain * states[1] + leakage * section_one
        section_three = retain * states[2] + leakage * section_two
        section_four = retain * states[3] + leakage * section_three
        return (jnp.stack([section_one, section_two, section_three, section_four]), section_four)
    anchor = jnp.zeros((4,) + fields.shape[:2], jnp.float32)
    if periodic:
        totals, unused = lax.scan(advance, anchor, inputs)
        anchor = periodic_start(transition(decays, fields.shape[2]), totals)
    unused, outputs = lax.scan(advance, anchor, inputs)
    outputs = jnp.moveaxis(outputs, 0, 2)
    if backward:
        outputs = outputs[:, :, ::-1]
    return outputs

def localize(fields, lon_decay, lat_decay):
    along_lon = filter_last(fields, lon_decay, True, False)
    across = filter_last(jnp.swapaxes(along_lon, 1, 2), lat_decay, False, False)
    return jnp.swapaxes(across, 1, 2)

def localize_adjoint(fields, lon_decay, lat_decay):
    across = filter_last(jnp.swapaxes(fields, 1, 2), lat_decay, False, True)
    return filter_last(jnp.swapaxes(across, 1, 2), lon_decay, True, True)

def reference(control, residual, direction, members, vert_modes, eig_count, lon_decay, lat_decay, obs_weight):
    mode_count = vert_modes.shape[0]
    member_count = eig_count.shape[0]
    active = (jnp.arange(mode_count)[None, :] < eig_count[:, None]).astype(jnp.float32)
    smooth = localize(direction, lon_decay, lat_decay)
    smooth = smooth.reshape(member_count, mode_count, NLAT, NLON) * active[:, :, None, None]

    def add_member(running, inputs):
        ensemble, weights = inputs
        profile = jnp.einsum('el,eyx->lyx', vert_modes, weights, precision=highest)
        return (running + ensemble.astype(jnp.float32) * profile, None)
    increment, unused = lax.scan(add_member, jnp.zeros((LEV, NLAT, NLON), jnp.float32), (members, smooth))
    weighted = obs_weight * increment

    def member_grad(carry, ensemble):
        projected = jnp.einsum('el,lyx->eyx', vert_modes, ensemble.astype(jnp.float32) * weighted, precision=highest)
        return (carry, projected)
    unused, gradient = lax.scan(member_grad, jnp.zeros((), jnp.float32), members)
    gradient = (gradient * active[:, :, None, None]).reshape(member_count * mode_count, NLAT, NLON)
    hessian = direction + localize_adjoint(gradient, lon_decay, lat_decay)
    norm_old = jnp.sum(residual * residual)
    curvature = jnp.sum(direction * hessian)
    step_size = norm_old / curvature
    new_control = control + step_size * direction
    new_residual = residual - step_size * hessian
    norm_new = jnp.sum(new_residual * new_residual)
    new_direction = new_residual + norm_new / norm_old * direction
    return (new_control, new_residual, new_direction)
```

```python
import functools

import jax
import jax.numpy as jnp
from jax import lax
from jax.experimental import pallas as pl
from jax.experimental.pallas import tpu as pltpu
from jax.sharding import PartitionSpec as P

MESH = pl.DeviceIdType.MESH
F32 = jnp.float32
BF16 = jnp.bfloat16

LON, LAT, MEM = 8, 8, 4
FIELDS, ROWS, COLS = 160, 8, 128
LEVELS, MODES = 32, 8
CHUNK = 16
CHUNKS = FIELDS // CHUNK
STATES = 4 * ROWS


def leak(c):
    series = jnp.ones_like(c)
    for k in range(10, 1, -1):
        series = 1.0 - (c / float(k)) * series
    return c * series


def rising(offset, degree):
    result = jnp.ones_like(offset)
    for k in range(degree):
        result = result * (offset + (k + 1.0)) * (1.0 / (k + 1.0))
    return result


def halves(x):
    high = x.astype(BF16)
    return high, (x - high.astype(F32)).astype(BF16)


def dot3(a, b, dims):
    dot = functools.partial(lax.dot_general, dimension_numbers=(dims, ((), ())), preferred_element_type=F32)
    return dot(a[0], b[0]) + (dot(a[0], b[1]) + dot(a[1], b[0]))


def iota(shape, dim):
    return lax.broadcasted_iota(jnp.int32, shape, dim)


def row_values(shape, lon_decay):
    row = iota(shape, 0)
    c = jnp.zeros(shape, F32)
    for y in range(ROWS):
        c = jnp.where(row // 4 == y, lon_decay[y], c)
    return row, c


def lon_gain(c):
    a = leak(c)
    return a * a * a * jnp.sqrt(a) * 2.5


def kernel(
    direction, residual, members, vert_modes, eig_count, lon_decay, lat_decay, obs_weight,
    hess_out, scal_out,
    dvm, rvm, mvm, ovm, nat, planes, kf_hi, kf_lo, kb_hi, kb_lo, vtab,
    lonc_f, lonc_b, lon_in, fin_f, fin_b, ent_f, ent_b,
    car_f, inc_f, car_b, inc_b, minc, weighted, red_a, red_b, red_c, tile,
    in_sem, out_sem, lon_s, lon_r, lat_s, lat_r, mem_s, mem_r, ra_s, ra_r, rb_s, rb_r, rc_s, rc_r,
):
    me_lon, me_lat, me_mem = lax.axis_index("lon"), lax.axis_index("lat"), lax.axis_index("mem")

    load_d = pltpu.make_async_copy(direction, dvm, in_sem.at[0])
    load_m = pltpu.make_async_copy(members, mvm, in_sem.at[1])
    load_o = pltpu.make_async_copy(obs_weight, ovm, in_sem.at[2])
    load_r = pltpu.make_async_copy(residual, rvm, in_sem.at[3])
    load_d.start()
    load_m.start()
    load_o.start()
    load_r.start()

    barrier = pltpu.get_barrier_semaphore()
    for axis, me, count in (("lon", me_lon, LON), ("lat", me_lat, LAT), ("mem", me_mem, MEM)):
        for delta in range(1, count):
            pl.semaphore_signal(
                barrier, inc=1, device_id={axis: lax.rem(me + delta, count)}, device_id_type=MESH
            )

    row, c_row = row_values((STATES, COLS), lon_decay)
    section = row % 4
    column = iota((STATES, COLS), 1).astype(F32)

    def pick(entries):
        result = entries[3]
        for s in range(3):
            result = jnp.where(section == s, entries[s], result)
        return result

    gain_row = lon_gain(c_row)
    last = COLS - 1.0
    fin_f[...] = pick([rising(last - column, s) for s in range(4)]) * jnp.exp(-(last - column) * c_row)
    fin_b[...] = pick([rising(column, s) for s in range(4)]) * jnp.exp(-column * c_row)
    ent_f[...] = (
        gain_row * pick([rising(column, 3 - s) for s in range(4)]) * jnp.exp(-(column + 1.0) * c_row)
    )
    ent_b[...] = (
        gain_row
        * pick([rising(last - column, 3 - s) for s in range(4)])
        * jnp.exp(-(last - column + 1.0) * c_row)
    )

    source = iota((COLS, COLS), 0)
    target = iota((COLS, COLS), 1)

    def response(offset, y):
        lag = jnp.maximum(offset, 0).astype(F32)
        c = jnp.full((COLS, COLS), lon_decay[y], F32)
        gain = lon_gain(jnp.full((8, COLS), lon_decay[y], F32))[0:1]
        return jnp.where(offset >= 0, rising(lag, 3) * gain * jnp.exp(-lag * c), 0.0)

    def tables_f(y, carry):
        kf_hi[y], kf_lo[y] = halves(response(target - source, y))
        return carry

    def tables_b(y, carry):
        kb_hi[y], kb_lo[y] = halves(response(source - target, y))
        return carry

    lax.fori_loop(0, ROWS, tables_f, 0)

    c_lat = lat_decay[...]
    q = jnp.broadcast_to(jnp.exp(-c_lat), (CHUNK, COLS))
    a_lat = leak(c_lat)
    gain_lat = jnp.broadcast_to(a_lat * a_lat * a_lat * jnp.sqrt(a_lat) * 2.5, (CHUNK, COLS))
    t0 = jnp.broadcast_to(jnp.exp(-8.0 * c_lat), (CHUNK, COLS))

    def lon_states(get_plane, fin, slots):
        total = jnp.zeros((STATES, FIELDS), F32)
        for y in range(ROWS):
            weights = jnp.where(row // 4 == y, fin[...], 0.0)
            total = total + dot3(halves(weights), halves(get_plane(y)), ((1,), (1,)))
        slots[pl.ds((LON - 1) * STATES, STATES), :] = total

    def lon_copy(slots, delta, phase):
        sign = 1 if phase == 0 else LON - 1
        return pltpu.make_async_remote_copy(
            src_ref=slots.at[pl.ds((LON - 1) * STATES, STATES)],
            dst_ref=slots.at[pl.ds((delta - 1) * STATES, STATES)],
            send_sem=lon_s.at[phase, delta - 1],
            recv_sem=lon_r.at[phase, delta - 1],
            device_id={"lon": lax.rem(me_lon + sign * delta, LON)},
            device_id_type=MESH,
        )

    def lon_incoming(slots):
        shape = (STATES, LON * STATES)
        to_row, c = row_values(shape, lon_decay)
        from_col = iota(shape, 1)
        same = (from_col % STATES) // 4 == to_row // 4
        spread = to_row % 4 - from_col % 4
        cells = ((from_col // STATES) * COLS).astype(F32)
        closing = jnp.exp(-cells * c)
        t = [closing * rising(cells - 1.0, k) for k in range(4)]
        circle = jnp.full(shape, float(COLS * LON), F32)
        closed = jnp.exp(-circle * c)
        n = [closed * rising(circle - 1.0, k) for k in range(4)]
        p = [1.0 / (1.0 - n[0])]
        p.append(p[0] * (n[1] * p[0]))
        p.append(p[0] * (n[1] * p[1] + n[2] * p[0]))
        p.append(p[0] * (n[1] * p[2] + n[2] * p[1] + n[3] * p[0]))
        m = [sum(t[j] * p[k - j] for j in range(k + 1)) for k in range(4)]
        mix = jnp.zeros(shape, F32)
        for k in range(4):
            mix = jnp.where(same & (spread == k), m[k], mix)
        incoming = dot3(halves(mix), halves(slots[...]), ((1,), (0,)))
        lon_in[...] = jnp.transpose(incoming)

    def enter(y, ent):
        weights = jnp.where(row // 4 == y, ent[...], 0.0)
        return dot3(halves(lon_in[...]), halves(weights), ((1,), (0,)))

    load_d.wait()

    def d_plane(y):
        return dvm[pl.ds(y, FIELDS, stride=ROWS), :]

    lon_states(d_plane, fin_f, lonc_f)
    pl.semaphore_wait(barrier, LON + LAT + MEM - 3)
    for delta in range(1, LON):
        lon_copy(lonc_f, delta, 0).start()

    def inside_f(y, carry):
        planes[y] = dot3(halves(d_plane(y)), (kf_hi[y], kf_lo[y]), ((1,), (0,)))
        return carry

    lax.fori_loop(0, ROWS, inside_f, 0)

    for delta in range(1, LON):
        lon_copy(lonc_f, delta, 0).wait_recv()
    lon_incoming(lonc_f)

    def entered_f(y):
        planes[y] = planes[y] + enter(y, ent_f)

    for y in range(ROWS):
        entered_f(y)

    def lat_copy(car, inc, c, phase):
        step = 1 if phase == 0 else LAT - 1
        return pltpu.make_async_remote_copy(
            src_ref=car.at[c],
            dst_ref=inc.at[c],
            send_sem=lat_s.at[phase, c],
            recv_sem=lat_r.at[phase, c],
            device_id={"lat": lax.rem(me_lat + step, LAT)},
            device_id_type=MESH,
        )

    def advance(v, f):
        v1 = q * v[0] + f
        v2 = q * v[1] + v1
        v3 = q * v[2] + v2
        v4 = q * v[3] + v3
        return [v1, v2, v3, v4]

    def own_states(get_row, order, car, c):
        v = [jnp.zeros((CHUNK, COLS), F32)] * 4
        for y in order:
            v = advance(v, get_row(y))
        for s in range(4):
            car[c, s] = v[s]

    def pass_on(car, inc, c):
        before = [inc[c, s] for s in range(4)]
        faded = [t0 * b for b in before]
        weight = (1.0, 8.0, 36.0, 120.0)
        for s in range(4):
            total = car[c, s] + faded[s]
            for j in range(s):
                total = total + weight[s - j] * faded[j]
            car[c, s] = total

    first, final = me_lat == 0, me_lat == LAT - 1

    def fields_of(c):
        return pl.ds(pl.multiple_of(c * CHUNK, CHUNK), CHUNK)

    def start_f(c, carry):
        own_states(lambda y: planes[y, fields_of(c), :], range(ROWS), car_f, c)

        @pl.when(first)
        def _():
            lat_copy(car_f, inc_f, c, 0).start()
            inc_f[c] = jnp.zeros((4, CHUNK, COLS), F32)

        return carry

    lax.fori_loop(0, CHUNKS, start_f, 0)

    for e in range(MODES):
        for l in range(LEVELS):
            vtab[l * MODES + e] = jnp.full((8, COLS), vert_modes[e, l], F32)
    lax.fori_loop(0, ROWS, tables_b, 0)
    load_m.wait()
    minc[me_mem] = jnp.zeros((LEVELS * ROWS, COLS), F32)

    lane_mode = iota((8, COLS), 0)

    def active(c):
        return jnp.concatenate(
            [
                jnp.where(lane_mode < eig_count[c * (CHUNK // MODES) + m], 1.0, 0.0)
                for m in range(CHUNK // MODES)
            ]
        )

    group = CHUNK // MODES

    def chain_f(c, carry):
        @pl.when(jnp.logical_not(first))
        def _():
            lat_copy(car_f, inc_f, c, 0).wait_recv()
            pass_on(car_f, inc_f, c)

            @pl.when(jnp.logical_not(final))
            def _():
                lat_copy(car_f, inc_f, c, 0).start()

        v = [inc_f[c, s] for s in range(4)]
        scale = gain_lat * active(c)
        for y in range(ROWS):
            v = advance(v, planes[y, fields_of(c), :])
            nat[pl.ds(c * (CHUNK * ROWS) + y, CHUNK, stride=ROWS), :] = v[3] * scale

        base = pl.multiple_of(c * (CHUNK * ROWS), CHUNK * ROWS)
        w = [nat[pl.ds(base + i * ROWS, ROWS), :] for i in range(CHUNK)]

        def levels(pair, carry):
            ens = [
                mvm[c * group + m, pl.ds(pl.multiple_of(pair * 16, 16), 16), :].astype(F32)
                for m in range(group)
            ]
            for h in range(2):
                total = None
                for m in range(group):
                    profile = None
                    for e in range(MODES):
                        term = vtab[(pair * 2 + h) * MODES + e] * w[m * MODES + e]
                        profile = term if profile is None else profile + term
                    term = ens[m][h * 8 : h * 8 + 8] * profile
                    total = term if total is None else total + term
                at = pl.ds(pl.multiple_of(pair * 16 + h * 8, 8), 8)
                minc[me_mem, at, :] = minc[me_mem, at, :] + total
            return carry

        lax.fori_loop(0, LEVELS // 2, levels, 0)
        return carry

    lax.fori_loop(0, CHUNKS, chain_f, 0)

    def mem_copy(delta):
        return pltpu.make_async_remote_copy(
            src_ref=minc.at[me_mem],
            dst_ref=minc.at[me_mem],
            send_sem=mem_s.at[delta - 1],
            recv_sem=mem_r.at[delta - 1],
            device_id={"mem": lax.rem(me_mem + delta, MEM)},
            device_id_type=MESH,
        )

    for delta in range(1, MEM):
        mem_copy(delta).start()
    load_o.wait()
    for delta in range(1, MEM):
        mem_copy(delta).wait_recv()
    weighted[...] = ovm[...] * ((minc[0] + minc[1]) + (minc[2] + minc[3]))

    def start_b(c, carry):
        def levels(pair, g):
            g = list(g)
            for m in range(group):
                ens = mvm[c * group + m, pl.ds(pl.multiple_of(pair * 16, 16), 16), :].astype(F32)
                both = ens * weighted[pl.ds(pl.multiple_of(pair * 16, 16), 16), :]
                for h in range(2):
                    for e in range(MODES):
                        g[m * MODES + e] = (
                            g[m * MODES + e]
                            + vtab[(pair * 2 + h) * MODES + e] * both[h * 8 : h * 8 + 8]
                        )
            return tuple(g)

        zero = jnp.zeros((8, COLS), F32)
        g = lax.fori_loop(0, LEVELS // 2, levels, (zero,) * CHUNK)
        base = pl.multiple_of(c * (CHUNK * ROWS), CHUNK * ROWS)
        for i in range(CHUNK):
            nat[pl.ds(base + i * ROWS, ROWS), :] = g[i]
        mask = active(c)
        for y in range(ROWS):
            planes[y, fields_of(c), :] = nat[pl.ds(c * (CHUNK * ROWS) + y, CHUNK, stride=ROWS), :] * mask
        own_states(lambda y: planes[y, fields_of(c), :], range(ROWS - 1, -1, -1), car_b, c)

        @pl.when(final)
        def _():
            lat_copy(car_b, inc_b, c, 1).start()
            inc_b[c] = jnp.zeros((4, CHUNK, COLS), F32)

        return carry

    lax.fori_loop(0, CHUNKS, start_b, 0)

    def chain_b(c, carry):
        @pl.when(jnp.logical_not(final))
        def _():
            lat_copy(car_b, inc_b, c, 1).wait_recv()
            pass_on(car_b, inc_b, c)

            @pl.when(jnp.logical_not(first))
            def _():
                lat_copy(car_b, inc_b, c, 1).start()

        v = [inc_b[c, s] for s in range(4)]
        for y in range(ROWS - 1, -1, -1):
            v = advance(v, planes[y, fields_of(c), :])
            planes[y, fields_of(c), :] = v[3] * gain_lat
        return carry

    lax.fori_loop(0, CHUNKS, chain_b, 0)

    lon_states(lambda y: planes[y], fin_b, lonc_b)
    for delta in range(1, LON):
        lon_copy(lonc_b, delta, 1).start()

    def inside_b(y, carry):
        planes[y] = dot3(halves(planes[y]), (kb_hi[y], kb_lo[y]), ((1,), (0,)))
        return carry

    lax.fori_loop(0, ROWS, inside_b, 0)
    load_r.wait()
    for delta in range(1, LON):
        lon_copy(lonc_b, delta, 1).wait_recv()
    lon_incoming(lonc_b)

    sums = [jnp.zeros((8, COLS), F32)] * 4

    def fold(x):
        return jnp.sum(x.reshape(FIELDS // 8, 8, COLS), axis=0)

    for y in range(ROWS):
        at = pl.ds(y, FIELDS, stride=ROWS)
        d, r = dvm[at, :], rvm[at, :]
        h = d + (planes[y] + enter(y, ent_b))
        nat[at, :] = h
        sums = [sums[0] + fold(r * r), sums[1] + fold(d * h), sums[2] + fold(r * h), sums[3] + fold(h * h)]
    store = pltpu.make_async_copy(nat, hess_out, out_sem.at[0])
    store.start()

    for k in range(4):
        tile[pl.ds(k, 1), :] = jnp.sum(sums[k], axis=0, keepdims=True)
    tile[pl.ds(4, 4), :] = jnp.zeros((4, COLS), F32)

    def reduce(axis, me, count, slots, s_sem, r_sem):
        slots[me] = tile[...]

        def copy(delta):
            return pltpu.make_async_remote_copy(
                src_ref=slots.at[me],
                dst_ref=slots.at[me],
                send_sem=s_sem.at[delta - 1],
                recv_sem=r_sem.at[delta - 1],
                device_id={axis: lax.rem(me + delta, count)},
                device_id_type=MESH,
            )

        for delta in range(1, count):
            copy(delta).start()
        for delta in range(1, count):
            copy(delta).wait_recv()
        total = slots[0]
        for k in range(1, count):
            total = total + slots[k]
        tile[...] = total
        return copy

    copy_a = reduce("lon", me_lon, LON, red_a, ra_s, ra_r)
    copy_b = reduce("mem", me_mem, MEM, red_b, rb_s, rb_r)
    copy_c = reduce("lat", me_lat, LAT, red_c, rc_s, rc_r)
    sums = jnp.broadcast_to(jnp.sum(tile[...], axis=1, keepdims=True), (8, COLS))
    rr, dh, rh, hh = (sums[k : k + 1] for k in range(4))
    step = rr / dh
    norm_new = rr - 2.0 * step * rh + step * step * hh
    scal_out[pl.ds(0, 1), :] = step
    scal_out[pl.ds(1, 1), :] = norm_new / rr
    scal_out[pl.ds(2, 6), :] = jnp.zeros((6, COLS), F32)

    store.wait()
    for delta in range(1, LON):
        lon_copy(lonc_f, delta, 0).wait_send()
        lon_copy(lonc_b, delta, 1).wait_send()
        copy_a(delta).wait_send()
    for delta in range(1, MEM):
        mem_copy(delta).wait_send()
        copy_b(delta).wait_send()
    for delta in range(1, LAT):
        copy_c(delta).wait_send()

    @pl.when(jnp.logical_not(final))
    def _():
        def left(c, carry):
            lat_copy(car_f, inc_f, c, 0).wait_send()
            return carry

        lax.fori_loop(0, CHUNKS, left, 0)

    @pl.when(jnp.logical_not(first))
    def _():
        def left(c, carry):
            lat_copy(car_b, inc_b, c, 1).wait_send()
            return carry

        lax.fori_loop(0, CHUNKS, left, 0)


def body(control, residual, direction, members, vert_modes, eig_count, lon_decay, lat_decay, obs_weight):
    rows = FIELDS * ROWS
    any_space = pl.BlockSpec(memory_space=pl.ANY)
    smem = pl.BlockSpec(memory_space=pltpu.SMEM)
    vmem = pl.BlockSpec(memory_space=pltpu.VMEM)
    dma = pltpu.SemaphoreType.DMA
    states = pltpu.VMEM((CHUNKS, 4, CHUNK, COLS), F32)
    table = pltpu.VMEM((ROWS, COLS, COLS), BF16)
    slots = pltpu.VMEM((LON * STATES, FIELDS), F32)
    small = pltpu.VMEM((STATES, COLS), F32)
    hessian, scalars = pl.pallas_call(
        kernel,
        name="cg_step",
        out_shape=(
            jax.ShapeDtypeStruct((rows, COLS), F32),
            jax.ShapeDtypeStruct((8, COLS), F32),
        ),
        in_specs=[any_space, any_space, any_space, smem, smem, smem, vmem, any_space],
        out_specs=(any_space, vmem),
        scratch_shapes=[
            pltpu.VMEM((rows, COLS), F32),
            pltpu.VMEM((rows, COLS), F32),
            pltpu.VMEM((FIELDS // MODES, LEVELS * ROWS, COLS), BF16),
            pltpu.VMEM((LEVELS * ROWS, COLS), F32),
            pltpu.VMEM((rows, COLS), F32),
            pltpu.VMEM((ROWS, FIELDS, COLS), F32),
            table, table, table, table,
            pltpu.VMEM((LEVELS * MODES, 8, COLS), F32),
            slots, slots,
            pltpu.VMEM((FIELDS, STATES), F32),
            small, small, small, small,
            states, states, states, states,
            pltpu.VMEM((MEM, LEVELS * ROWS, COLS), F32),
            pltpu.VMEM((LEVELS * ROWS, COLS), F32),
            pltpu.VMEM((LON, 8, COLS), F32),
            pltpu.VMEM((MEM, 8, COLS), F32),
            pltpu.VMEM((LAT, 8, COLS), F32),
            pltpu.VMEM((8, COLS), F32),
            dma((4,)), dma((1,)),
            dma((2, LON - 1)), dma((2, LON - 1)),
            dma((2, CHUNKS)), dma((2, CHUNKS)),
            dma((MEM - 1,)), dma((MEM - 1,)),
            dma((LON - 1,)), dma((LON - 1,)),
            dma((MEM - 1,)), dma((MEM - 1,)),
            dma((LAT - 1,)), dma((LAT - 1,)),
        ],
        compiler_params=pltpu.CompilerParams(
            collective_id=0, has_side_effects=True, vmem_limit_bytes=60 << 20
        ),
    )(
        direction.reshape(rows, COLS),
        residual.reshape(rows, COLS),
        members.reshape(FIELDS // MODES, LEVELS * ROWS, COLS),
        vert_modes,
        eig_count,
        lon_decay,
        lat_decay.reshape(1, COLS),
        obs_weight.reshape(LEVELS * ROWS, COLS),
    )
    hessian = hessian.reshape(direction.shape)
    step, ratio = scalars[0, 0], scalars[1, 0]
    new_control = control + step * direction
    new_residual = residual - step * hessian
    new_direction = new_residual + ratio * direction
    return new_control, new_residual, new_direction


def solution(mesh):
    field = P("mem", "lat", "lon")
    placed = (
        field, field, field, P("mem", None, "lat", "lon"), P(), P("mem"), P("lat"), P("lon"),
        P(None, "lat", "lon"),
    )
    return jax.shard_map(
        body, mesh=mesh, in_specs=placed, out_specs=(field, field, field), check_vma=False
    )
```

```python
import functools

import jax
import jax.numpy as jnp
from jax import lax
from jax.experimental import pallas as pl
from jax.experimental.pallas import tpu as pltpu
from jax.sharding import PartitionSpec as P

MESH = pl.DeviceIdType.MESH
F32 = jnp.float32
BF16 = jnp.bfloat16

LON, LAT, MEM = 8, 8, 4
FIELDS, ROWS, COLS = 160, 8, 128
LEVELS, MODES = 32, 8
CHUNK = 8
GROUP = 2
LAG = 6
CHUNKS = FIELDS // CHUNK
STATES = 4 * ROWS


def leak(c):
    series = jnp.ones_like(c)
    for k in range(10, 1, -1):
        series = 1.0 - (c / float(k)) * series
    return c * series


def rising(offset, degree):
    result = jnp.ones_like(offset)
    for k in range(degree):
        result = result * (offset + (k + 1.0)) * (1.0 / (k + 1.0))
    return result


def halves(x):
    high = x.astype(BF16)
    return high, (x - high.astype(F32)).astype(BF16)


def dot3(a, b, dims):
    dot = functools.partial(lax.dot_general, dimension_numbers=(dims, ((), ())), preferred_element_type=F32)
    return dot(a[0], b[0]) + (dot(a[0], b[1]) + dot(a[1], b[0]))


def iota(shape, dim):
    return lax.broadcasted_iota(jnp.int32, shape, dim)


def row_values(shape, lon_decay):
    row = iota(shape, 0)
    c = jnp.zeros(shape, F32)
    for y in range(ROWS):
        c = jnp.where(row // 4 == y, lon_decay[y], c)
    return row, c


def lon_gain(c):
    a = leak(c)
    return a * a * a * jnp.sqrt(a) * 2.5


def kernel(
    direction, residual, members, vert_modes, eig_count, lon_decay, lat_decay, obs_weight,
    hess_out, step_out, ratio_out,
    dvm, rvm, mvm, ovm, nat, planes, kf_hi, kf_lo, kb_hi, kb_lo, vtab,
    lonc_f, lonc_b, lon_in, fin_f, fin_b, ent_f, ent_b,
    lat_f, lat_b, minc, weighted, red_a, red_b, red_c, tile,
    in_sem, out_sem, lon_s, lon_r, lat_s, lat_r, mem_s, mem_r, ra_s, ra_r, rb_s, rb_r, rc_s, rc_r,
):
    me_lon, me_lat, me_mem = lax.axis_index("lon"), lax.axis_index("lat"), lax.axis_index("mem")

    load_d = pltpu.make_async_copy(direction, dvm, in_sem.at[0])
    load_m = pltpu.make_async_copy(members, mvm, in_sem.at[1])
    load_o = pltpu.make_async_copy(obs_weight, ovm, in_sem.at[2])
    load_r = pltpu.make_async_copy(residual, rvm, in_sem.at[3])
    load_d.start()
    load_m.start()
    load_o.start()
    load_r.start()

    barrier = pltpu.get_barrier_semaphore()
    for axis, me, count in (("lon", me_lon, LON), ("lat", me_lat, LAT), ("mem", me_mem, MEM)):
        for delta in (1, LAT - 1) if axis == "lat" else range(1, count):
            pl.semaphore_signal(
                barrier, inc=1, device_id={axis: lax.rem(me + delta, count)}, device_id_type=MESH
            )

    row, c_row = row_values((STATES, COLS), lon_decay)
    section = row % 4
    column = iota((STATES, COLS), 1).astype(F32)

    def pick(entries):
        result = entries[3]
        for s in range(3):
            result = jnp.where(section == s, entries[s], result)
        return result

    gain_row = lon_gain(c_row)
    last = COLS - 1.0
    fin_f[...] = pick([rising(last - column, s) for s in range(4)]) * jnp.exp(-(last - column) * c_row)
    fin_b[...] = pick([rising(column, s) for s in range(4)]) * jnp.exp(-column * c_row)
    ent_f[...] = (
        gain_row * pick([rising(column, 3 - s) for s in range(4)]) * jnp.exp(-(column + 1.0) * c_row)
    )
    ent_b[...] = (
        gain_row
        * pick([rising(last - column, 3 - s) for s in range(4)])
        * jnp.exp(-(last - column + 1.0) * c_row)
    )

    source = iota((COLS, COLS), 0)
    target = iota((COLS, COLS), 1)

    def response(offset, y):
        lag = jnp.maximum(offset, 0).astype(F32)
        c = jnp.full((COLS, COLS), lon_decay[y], F32)
        gain = lon_gain(jnp.full((8, COLS), lon_decay[y], F32))[0:1]
        return jnp.where(offset >= 0, rising(lag, 3) * gain * jnp.exp(-lag * c), 0.0)

    def tables_f(y, carry):
        kf_hi[y], kf_lo[y] = halves(response(target - source, y))
        return carry

    def tables_b(y, carry):
        kb_hi[y], kb_lo[y] = halves(response(source - target, y))
        return carry

    lax.fori_loop(0, ROWS, tables_f, 0)

    c_lat = lat_decay[...]
    q = jnp.broadcast_to(jnp.exp(-c_lat), (CHUNK, COLS))
    a_lat = leak(c_lat)
    gain_lat = jnp.broadcast_to(a_lat * a_lat * a_lat * jnp.sqrt(a_lat) * 2.5, (CHUNK, COLS))

    def lon_states(get_plane, fin, slots):
        total = jnp.zeros((STATES, FIELDS), F32)
        for y in range(ROWS):
            weights = jnp.where(row // 4 == y, fin[...], 0.0)
            total = total + dot3(halves(weights), halves(get_plane(y)), ((1,), (1,)))
        slots[pl.ds((LON - 1) * STATES, STATES), :] = total

    def lon_copy(slots, delta, phase):
        sign = 1 if phase == 0 else LON - 1
        return pltpu.make_async_remote_copy(
            src_ref=slots.at[pl.ds((LON - 1) * STATES, STATES)],
            dst_ref=slots.at[pl.ds((delta - 1) * STATES, STATES)],
            send_sem=lon_s.at[phase, delta - 1],
            recv_sem=lon_r.at[phase, delta - 1],
            device_id={"lon": lax.rem(me_lon + sign * delta, LON)},
            device_id_type=MESH,
        )

    def lon_incoming(slots):
        shape = (STATES, LON * STATES)
        to_row, c = row_values(shape, lon_decay)
        from_col = iota(shape, 1)
        same = (from_col % STATES) // 4 == to_row // 4
        spread = to_row % 4 - from_col % 4
        cells = ((from_col // STATES) * COLS).astype(F32)
        closing = jnp.exp(-cells * c)
        t = [closing * rising(cells - 1.0, k) for k in range(4)]
        circle = jnp.full(shape, float(COLS * LON), F32)
        closed = jnp.exp(-circle * c)
        n = [closed * rising(circle - 1.0, k) for k in range(4)]
        p = [1.0 / (1.0 - n[0])]
        p.append(p[0] * (n[1] * p[0]))
        p.append(p[0] * (n[1] * p[1] + n[2] * p[0]))
        p.append(p[0] * (n[1] * p[2] + n[2] * p[1] + n[3] * p[0]))
        m = [sum(t[j] * p[k - j] for j in range(k + 1)) for k in range(4)]
        mix = jnp.zeros(shape, F32)
        for k in range(4):
            mix = jnp.where(same & (spread == k), m[k], mix)
        incoming = dot3(halves(mix), halves(slots[...]), ((1,), (0,)))
        lon_in[...] = jnp.transpose(incoming)

    def enter(y, ent):
        weights = jnp.where(row // 4 == y, ent[...], 0.0)
        return dot3(halves(lon_in[...]), halves(weights), ((1,), (0,)))

    load_d.wait()

    def d_plane(y):
        return dvm[pl.ds(y, FIELDS, stride=ROWS), :]

    lon_states(d_plane, fin_f, lonc_f)
    pl.semaphore_wait(barrier, LON - 1 + 2 + MEM - 1)
    for delta in range(1, LON):
        lon_copy(lonc_f, delta, 0).start()

    def inside_f(y, carry):
        planes[y] = dot3(halves(d_plane(y)), (kf_hi[y], kf_lo[y]), ((1,), (0,)))
        return carry

    lax.fori_loop(0, ROWS, inside_f, 0)

    for delta in range(1, LON):
        lon_copy(lonc_f, delta, 0).wait_recv()
    lon_incoming(lonc_f)

    def entered_f(y):
        planes[y] = planes[y] + enter(y, ent_f)

    for y in range(ROWS):
        entered_f(y)

    OWN, AHEAD_IN, TOTAL_IN, AHEAD_OUT, TOTAL_OUT = range(5)

    def lat_copy(bufs, phase, c, source, ahead, step):
        sign = step if phase == 0 else -step
        stream = 0 if ahead else 1
        return pltpu.make_async_remote_copy(
            src_ref=bufs.at[source, c],
            dst_ref=bufs.at[AHEAD_IN if ahead else TOTAL_IN, c],
            send_sem=lat_s.at[phase, stream, c],
            recv_sem=lat_r.at[phase, stream, c],
            device_id={"lat": lax.rem(me_lat + (LAT + sign), LAT)},
            device_id_type=MESH,
        )

    def advance(v, f):
        v1 = q * v[0] + f
        v2 = q * v[1] + v1
        v3 = q * v[2] + v2
        v4 = q * v[3] + v3
        return [v1, v2, v3, v4]

    def own_states(get_row, order, bufs, c):
        v = [jnp.zeros((CHUNK, COLS), F32)] * 4
        for y in order:
            v = advance(v, get_row(y))
        for s in range(4):
            bufs[OWN, c, s] = v[s]

    def transition(cells):
        closing = jnp.exp(-cells * c_lat)
        offset = jnp.zeros((1, COLS), F32) + (cells - 1.0)
        return [jnp.broadcast_to(closing * rising(offset, k), (CHUNK, COLS)) for k in range(4)]

    one_block = transition(float(ROWS))

    def add_moved(move, moved, fixed, result, bufs, c):
        v = [bufs[moved, c, s] for s in range(4)]
        w = [bufs[fixed, c, s] for s in range(4)]
        for s in range(4):
            total = w[s]
            for j in range(s + 1):
                total = total + move[s - j] * v[j]
            bufs[result, c, s] = total

    def is_in(p, *places):
        return functools.reduce(jnp.logical_or, [p == k for k in places])

    def places_of(phase):
        p = me_lat if phase == 0 else LAT - 1 - me_lat
        blocks = jnp.where(p < 4, 3 - p, p - 4)
        return p, transition((blocks * ROWS).astype(F32))

    def lat_begin(bufs, phase, p, c):
        @pl.when(is_in(p, 0, 4))
        def _():
            lat_copy(bufs, phase, c, OWN, True, 1).start()

        @pl.when(p == 3)
        def _():
            lat_copy(bufs, phase, c, OWN, False, -1).start()

        @pl.when(p == 0)
        def _():
            bufs[AHEAD_IN, c] = jnp.zeros((4, CHUNK, COLS), F32)

    def lat_streams(bufs, phase, p, far):
        late_ahead = jnp.where(p == 2, LAG, 0)
        late_total = jnp.where(p == 1, LAG, 0)

        def step(t, carry):
            a, b = t - late_ahead, t - late_total

            @pl.when(is_in(p, 1, 2, 3, 5, 6) & (a >= 0) & (a < CHUNKS))
            def _():
                lat_copy(bufs, phase, a, AHEAD_OUT, True, 1).wait_recv()
                add_moved(one_block, AHEAD_IN, OWN, AHEAD_OUT, bufs, a)
                lat_copy(bufs, phase, a, AHEAD_OUT, True, 1).start()

            @pl.when((p < 3) & (b >= 0) & (b < CHUNKS))
            def _():
                lat_copy(bufs, phase, b, TOTAL_OUT, False, -1).wait_recv()
                add_moved(far, OWN, TOTAL_IN, TOTAL_OUT, bufs, b)
                lat_copy(bufs, phase, b, TOTAL_OUT, False, -1).start()

            return carry

        lax.fori_loop(0, CHUNKS + LAG, step, 0)

    def lat_finish(bufs, phase, p, far, c):
        @pl.when(is_in(p, 4, 7))
        def _():
            lat_copy(bufs, phase, c, AHEAD_OUT, True, 1).wait_recv()

        @pl.when(p == 4)
        def _():
            lat_copy(bufs, phase, c, AHEAD_IN, False, 1).start()

        @pl.when(p > 4)
        def _():
            lat_copy(bufs, phase, c, TOTAL_OUT, False, -1).wait_recv()

        @pl.when(p == 7)
        def _():
            lat_copy(bufs, phase, c, TOTAL_IN, False, -1).start()

        @pl.when(p > 4)
        def _():
            add_moved(far, TOTAL_IN, AHEAD_IN, AHEAD_IN, bufs, c)

        return [bufs[AHEAD_IN, c, s] for s in range(4)]

    def lat_left(bufs, phase, p):
        def left(c, carry):
            @pl.when(p < 7)
            def _():
                lat_copy(bufs, phase, c, AHEAD_OUT, True, 1).wait_send()

            @pl.when((p < 5) | (p == 7))
            def _():
                lat_copy(bufs, phase, c, TOTAL_OUT, False, -1).wait_send()

            return carry

        lax.fori_loop(0, CHUNKS, left, 0)

    p_f, far_f = places_of(0)
    p_b, far_b = places_of(1)

    def fields_of(c):
        return pl.ds(pl.multiple_of(c * CHUNK, CHUNK), CHUNK)

    def start_f(c, carry):
        own_states(lambda y: planes[y, fields_of(c), :], range(ROWS), lat_f, c)
        lat_begin(lat_f, 0, p_f, c)
        return carry

    lax.fori_loop(0, CHUNKS, start_f, 0)

    for e in range(MODES):
        for l in range(LEVELS):
            vtab[l * MODES + e] = jnp.full((8, COLS), vert_modes[e, l], F32)
    lax.fori_loop(0, ROWS, tables_b, 0)
    load_m.wait()
    minc[me_mem] = jnp.zeros((LEVELS * ROWS, COLS), F32)

    mode = iota((CHUNK, COLS), 0)

    def active(c):
        return jnp.where(mode < eig_count[c], 1.0, 0.0)

    lat_streams(lat_f, 0, p_f, far_f)

    def chain_f(g, carry):
        w = []
        for k in range(GROUP):
            c = g * GROUP + k
            v = lat_finish(lat_f, 0, p_f, far_f, c)
            scale = gain_lat * active(c)
            for y in range(ROWS):
                v = advance(v, planes[y, fields_of(c), :])
                nat[pl.ds(c * (CHUNK * ROWS) + y, CHUNK, stride=ROWS), :] = v[3] * scale
            base = pl.multiple_of(c * (CHUNK * ROWS), CHUNK * ROWS)
            w.append([nat[pl.ds(base + e * ROWS, ROWS), :] for e in range(MODES)])

        def levels(pair, carry):
            at = pl.ds(pl.multiple_of(pair * 16, 16), 16)
            ens = [mvm[g * GROUP + m, at, :].astype(F32) for m in range(GROUP)]
            for h in range(2):
                total = None
                for m in range(GROUP):
                    profile = None
                    for e in range(MODES):
                        term = vtab[(pair * 2 + h) * MODES + e] * w[m][e]
                        profile = term if profile is None else profile + term
                    term = ens[m][h * 8 : h * 8 + 8] * profile
                    total = term if total is None else total + term
                at = pl.ds(pl.multiple_of(pair * 16 + h * 8, 8), 8)
                minc[me_mem, at, :] = minc[me_mem, at, :] + total
            return carry

        lax.fori_loop(0, LEVELS // 2, levels, 0)
        return carry

    lax.fori_loop(0, CHUNKS // GROUP, chain_f, 0)

    def mem_copy(delta):
        return pltpu.make_async_remote_copy(
            src_ref=minc.at[me_mem],
            dst_ref=minc.at[me_mem],
            send_sem=mem_s.at[delta - 1],
            recv_sem=mem_r.at[delta - 1],
            device_id={"mem": lax.rem(me_mem + delta, MEM)},
            device_id_type=MESH,
        )

    for delta in range(1, MEM):
        mem_copy(delta).start()
    load_o.wait()
    for delta in range(1, MEM):
        mem_copy(delta).wait_recv()
    weighted[...] = ovm[...] * ((minc[0] + minc[1]) + (minc[2] + minc[3]))

    def start_b(g, carry):
        def levels(pair, total):
            total = list(total)
            at = pl.ds(pl.multiple_of(pair * 16, 16), 16)
            weight = weighted[at, :]
            for m in range(GROUP):
                both = mvm[g * GROUP + m, at, :].astype(F32) * weight
                for h in range(2):
                    for e in range(MODES):
                        total[m * MODES + e] = (
                            total[m * MODES + e]
                            + vtab[(pair * 2 + h) * MODES + e] * both[h * 8 : h * 8 + 8]
                        )
            return tuple(total)

        zero = jnp.zeros((8, COLS), F32)
        total = lax.fori_loop(0, LEVELS // 2, levels, (zero,) * (GROUP * MODES))
        for k in range(GROUP):
            c = g * GROUP + k
            base = pl.multiple_of(c * (CHUNK * ROWS), CHUNK * ROWS)
            for e in range(MODES):
                nat[pl.ds(base + e * ROWS, ROWS), :] = total[k * MODES + e]
            mask = active(c)
            for y in range(ROWS):
                planes[y, fields_of(c), :] = (
                    nat[pl.ds(c * (CHUNK * ROWS) + y, CHUNK, stride=ROWS), :] * mask
                )
            own_states(lambda y: planes[y, fields_of(c), :], range(ROWS - 1, -1, -1), lat_b, c)
            lat_begin(lat_b, 1, p_b, c)
        return carry

    lax.fori_loop(0, CHUNKS // GROUP, start_b, 0)
    lat_streams(lat_b, 1, p_b, far_b)

    def chain_b(c, carry):
        v = lat_finish(lat_b, 1, p_b, far_b, c)
        for y in range(ROWS - 1, -1, -1):
            v = advance(v, planes[y, fields_of(c), :])
            planes[y, fields_of(c), :] = v[3] * gain_lat
        return carry

    lax.fori_loop(0, CHUNKS, chain_b, 0)

    lon_states(lambda y: planes[y], fin_b, lonc_b)
    for delta in range(1, LON):
        lon_copy(lonc_b, delta, 1).start()

    def inside_b(y, carry):
        planes[y] = dot3(halves(planes[y]), (kb_hi[y], kb_lo[y]), ((1,), (0,)))
        return carry

    lax.fori_loop(0, ROWS, inside_b, 0)
    load_r.wait()
    for delta in range(1, LON):
        lon_copy(lonc_b, delta, 1).wait_recv()
    lon_incoming(lonc_b)

    sums = [jnp.zeros((8, COLS), F32)] * 4

    def fold(x):
        return jnp.sum(x.reshape(FIELDS // 8, 8, COLS), axis=0)

    for y in range(ROWS):
        at = pl.ds(y, FIELDS, stride=ROWS)
        d, r = dvm[at, :], rvm[at, :]
        h = d + (planes[y] + enter(y, ent_b))
        nat[at, :] = h
        sums = [sums[0] + fold(r * r), sums[1] + fold(d * h), sums[2] + fold(r * h), sums[3] + fold(h * h)]
    store = pltpu.make_async_copy(nat, hess_out, out_sem.at[0])
    store.start()

    for k in range(4):
        tile[pl.ds(k, 1), :] = jnp.sum(sums[k], axis=0, keepdims=True)
    tile[pl.ds(4, 4), :] = jnp.zeros((4, COLS), F32)

    def reduce(axis, me, count, slots, s_sem, r_sem):
        slots[me] = tile[...]

        def copy(delta):
            return pltpu.make_async_remote_copy(
                src_ref=slots.at[me],
                dst_ref=slots.at[me],
                send_sem=s_sem.at[delta - 1],
                recv_sem=r_sem.at[delta - 1],
                device_id={axis: lax.rem(me + delta, count)},
                device_id_type=MESH,
            )

        for delta in range(1, count):
            copy(delta).start()
        for delta in range(1, count):
            copy(delta).wait_recv()
        total = slots[0]
        for k in range(1, count):
            total = total + slots[k]
        tile[...] = total
        return copy

    copy_a = reduce("lon", me_lon, LON, red_a, ra_s, ra_r)
    copy_b = reduce("mem", me_mem, MEM, red_b, rb_s, rb_r)
    copy_c = reduce("lat", me_lat, LAT, red_c, rc_s, rc_r)
    sums = jnp.broadcast_to(jnp.sum(tile[...], axis=1, keepdims=True), (8, COLS))
    rr, dh, rh, hh = (sums[k : k + 1] for k in range(4))
    step = rr / dh
    norm_new = rr - 2.0 * step * rh + step * step * hh
    step_out[0, 0] = step[0, 0]
    ratio_out[0, 0] = (norm_new / rr)[0, 0]

    store.wait()
    for delta in range(1, LON):
        lon_copy(lonc_f, delta, 0).wait_send()
        lon_copy(lonc_b, delta, 1).wait_send()
        copy_a(delta).wait_send()
    for delta in range(1, MEM):
        mem_copy(delta).wait_send()
        copy_b(delta).wait_send()
    for delta in range(1, LAT):
        copy_c(delta).wait_send()

    lat_left(lat_f, 0, p_f)
    lat_left(lat_b, 1, p_b)


def body(control, residual, direction, members, vert_modes, eig_count, lon_decay, lat_decay, obs_weight):
    rows = FIELDS * ROWS
    any_space = pl.BlockSpec(memory_space=pl.ANY)
    smem = pl.BlockSpec(memory_space=pltpu.SMEM)
    vmem = pl.BlockSpec(memory_space=pltpu.VMEM)
    dma = pltpu.SemaphoreType.DMA
    states = pltpu.VMEM((5, CHUNKS, 4, CHUNK, COLS), F32)
    table = pltpu.VMEM((ROWS, COLS, COLS), BF16)
    slots = pltpu.VMEM((LON * STATES, FIELDS), F32)
    small = pltpu.VMEM((STATES, COLS), F32)
    one = jax.ShapeDtypeStruct((1, 1), F32)
    hessian, step, ratio = pl.pallas_call(
        kernel,
        name="cg_step",
        out_shape=(
            jax.ShapeDtypeStruct((rows, COLS), F32),
            one, one,
        ),
        in_specs=[any_space, any_space, any_space, smem, smem, smem, vmem, any_space],
        out_specs=(any_space, smem, smem),
        scratch_shapes=[
            pltpu.VMEM((rows, COLS), F32),
            pltpu.VMEM((rows, COLS), F32),
            pltpu.VMEM((FIELDS // MODES, LEVELS * ROWS, COLS), BF16),
            pltpu.VMEM((LEVELS * ROWS, COLS), F32),
            pltpu.VMEM((rows, COLS), F32),
            pltpu.VMEM((ROWS, FIELDS, COLS), F32),
            table, table, table, table,
            pltpu.VMEM((LEVELS * MODES, 8, COLS), F32),
            slots, slots,
            pltpu.VMEM((FIELDS, STATES), F32),
            small, small, small, small,
            states, states,
            pltpu.VMEM((MEM, LEVELS * ROWS, COLS), F32),
            pltpu.VMEM((LEVELS * ROWS, COLS), F32),
            pltpu.VMEM((LON, 8, COLS), F32),
            pltpu.VMEM((MEM, 8, COLS), F32),
            pltpu.VMEM((LAT, 8, COLS), F32),
            pltpu.VMEM((8, COLS), F32),
            dma((4,)), dma((1,)),
            dma((2, LON - 1)), dma((2, LON - 1)),
            dma((2, 2, CHUNKS)), dma((2, 2, CHUNKS)),
            dma((MEM - 1,)), dma((MEM - 1,)),
            dma((LON - 1,)), dma((LON - 1,)),
            dma((MEM - 1,)), dma((MEM - 1,)),
            dma((LAT - 1,)), dma((LAT - 1,)),
        ],
        compiler_params=pltpu.CompilerParams(
            collective_id=0, has_side_effects=True, vmem_limit_bytes=60 << 20
        ),
    )(
        direction.reshape(rows, COLS),
        residual.reshape(rows, COLS),
        members.reshape(FIELDS // MODES, LEVELS * ROWS, COLS),
        vert_modes,
        eig_count,
        lon_decay,
        lat_decay.reshape(1, COLS),
        obs_weight.reshape(LEVELS * ROWS, COLS),
    )
    hessian = hessian.reshape(direction.shape)
    step, ratio = step.reshape(()), ratio.reshape(())
    new_control = control + step * direction
    new_residual = residual - step * hessian
    new_direction = new_residual + ratio * direction
    return new_control, new_residual, new_direction


def solution(mesh):
    field = P("mem", "lat", "lon")
    placed = (
        field, field, field, P("mem", None, "lat", "lon"), P(), P("mem"), P("lat"), P("lon"),
        P(None, "lat", "lon"),
    )
    return jax.shard_map(
        body, mesh=mesh, in_specs=placed, out_specs=(field, field, field), check_vma=False
    )
```

```python
import functools

import jax
import jax.numpy as jnp
from jax import lax
from jax.experimental import pallas as pl
from jax.experimental.pallas import tpu as pltpu
from jax.sharding import PartitionSpec as P

MESH = pl.DeviceIdType.MESH
F32 = jnp.float32
BF16 = jnp.bfloat16

LON, LAT, MEM = 8, 8, 4
FIELDS, ROWS, COLS = 160, 8, 128
LEVELS, MODES = 32, 8
CHUNK = 8
GROUP = 2
LAG = 12
CHUNKS = FIELDS // CHUNK
GROUPS = ((128, 32), (0, 128))
FIRST = 16
STATES = 4 * ROWS


def leak(c):
    series = jnp.ones_like(c)
    for k in range(10, 1, -1):
        series = 1.0 - (c / float(k)) * series
    return c * series


def rising(offset, degree):
    result = jnp.ones_like(offset)
    for k in range(degree):
        result = result * (offset + (k + 1.0)) * (1.0 / (k + 1.0))
    return result


def halves(x):
    high = x.astype(BF16)
    return high, (x - high.astype(F32)).astype(BF16)


def dot3(a, b, dims):
    dot = functools.partial(lax.dot_general, dimension_numbers=(dims, ((), ())), preferred_element_type=F32)
    return dot(a[0], b[0]) + (dot(a[0], b[1]) + dot(a[1], b[0]))


def iota(shape, dim):
    return lax.broadcasted_iota(jnp.int32, shape, dim)


def row_values(shape, lon_decay):
    row = iota(shape, 0)
    c = jnp.zeros(shape, F32)
    for y in range(ROWS):
        c = jnp.where(row // 4 == y, lon_decay[y], c)
    return row, c


def lon_gain(c):
    a = leak(c)
    return a * a * a * jnp.sqrt(a) * 2.5


def kernel(
    direction, residual, members, vert_modes_in, eig_count_in, lon_decay_in, lat_decay_in, obs_weight,
    hess_out, step_out, ratio_out,
    vert_modes, eig_count, lon_decay, lat_decay, dvm, rvm, mvm, ovm, nat, planes, kf_hi, kf_lo, kb_hi, kb_lo, vtab,
    lon_fa, lon_fb, lon_ba, lon_bb, in_a, in_b, mix_hi, mix_lo, fin_f, fin_b, ent_f, ent_b,
    lat_f, lat_b, minc, weighted, red_a, red_c, tile,
    in_sem, out_sem, lon_s, lon_r, lat_s, lat_r, mem_s, mem_r, ra_s, ra_r, rc_s, rc_r,
):
    me_lon, me_lat, me_mem = lax.axis_index("lon"), lax.axis_index("lat"), lax.axis_index("mem")

    barrier = pltpu.get_barrier_semaphore()
    for axis, me, count in (("lon", me_lon, LON), ("lat", me_lat, LAT), ("mem", me_mem, MEM)):
        for delta in (1, LAT - 1) if axis == "lat" else range(1, count):
            pl.semaphore_signal(
                barrier, inc=1, device_id={axis: lax.rem(me + delta, count)}, device_id_type=MESH
            )

    load_d = pltpu.make_async_copy(direction, dvm, in_sem.at[0])
    load_m = pltpu.make_async_copy(members, mvm, in_sem.at[1])
    load_o = pltpu.make_async_copy(obs_weight, ovm, in_sem.at[2])
    load_r = pltpu.make_async_copy(residual, rvm, in_sem.at[3])
    small = [
        pltpu.make_async_copy(lon_decay_in, lon_decay, in_sem.at[4]),
        pltpu.make_async_copy(lat_decay_in, lat_decay, in_sem.at[5]),
        pltpu.make_async_copy(vert_modes_in, vert_modes, in_sem.at[6]),
        pltpu.make_async_copy(eig_count_in, eig_count, in_sem.at[7]),
    ]
    for load in (*small, load_d, load_m, load_o, load_r):
        load.start()
    for load in small:
        load.wait()

    row, c_row = row_values((STATES, COLS), lon_decay)
    section = row % 4
    column = iota((STATES, COLS), 1).astype(F32)

    def pick(entries):
        result = entries[3]
        for s in range(3):
            result = jnp.where(section == s, entries[s], result)
        return result

    gain_row = lon_gain(c_row)
    last = COLS - 1.0
    fin_f[...] = pick([rising(last - column, s) for s in range(4)]) * jnp.exp(-(last - column) * c_row)
    fin_b[...] = pick([rising(column, s) for s in range(4)]) * jnp.exp(-column * c_row)
    ent_f[...] = (
        gain_row * pick([rising(column, 3 - s) for s in range(4)]) * jnp.exp(-(column + 1.0) * c_row)
    )
    ent_b[...] = (
        gain_row
        * pick([rising(last - column, 3 - s) for s in range(4)])
        * jnp.exp(-(last - column + 1.0) * c_row)
    )

    source = iota((COLS, COLS), 0)
    target = iota((COLS, COLS), 1)

    def response(offset, y):
        lag = jnp.maximum(offset, 0).astype(F32)
        c = jnp.full((COLS, COLS), lon_decay[y], F32)
        gain = lon_gain(jnp.full((8, COLS), lon_decay[y], F32))[0:1]
        return jnp.where(offset >= 0, rising(lag, 3) * gain * jnp.exp(-lag * c), 0.0)

    def tables_f(y, carry):
        kf_hi[y], kf_lo[y] = halves(response(target - source, y))
        return carry

    def tables_b(y, carry):
        kb_hi[y], kb_lo[y] = halves(response(source - target, y))
        return carry

    lax.fori_loop(0, ROWS, tables_f, 0)

    c_lat = lat_decay[...]
    q = jnp.broadcast_to(jnp.exp(-c_lat), (CHUNK, COLS))
    a_lat = leak(c_lat)
    gain_lat = jnp.broadcast_to(a_lat * a_lat * a_lat * jnp.sqrt(a_lat) * 2.5, (CHUNK, COLS))

    lon_slots = ((lon_fa, lon_fb), (lon_ba, lon_bb))
    lon_in = (in_a, in_b)

    def lon_states(get_plane, fin, phase, g):
        first, count = GROUPS[g]
        total = jnp.zeros((STATES, count), F32)
        for y in range(ROWS):
            weights = jnp.where(row // 4 == y, fin[...], 0.0)
            total = total + dot3(halves(weights), halves(get_plane(y, first, count)), ((1,), (1,)))
        lon_slots[phase][g][pl.ds((LON - 1) * STATES, STATES), :] = total

    def lon_copy(phase, g, delta):
        sign = 1 if phase == 0 else LON - 1
        slots = lon_slots[phase][g]
        return pltpu.make_async_remote_copy(
            src_ref=slots.at[pl.ds((LON - 1) * STATES, STATES)],
            dst_ref=slots.at[pl.ds((delta - 1) * STATES, STATES)],
            send_sem=lon_s.at[phase, g, delta - 1],
            recv_sem=lon_r.at[phase, g, delta - 1],
            device_id={"lon": lax.rem(me_lon + sign * delta, LON)},
            device_id_type=MESH,
        )

    def lon_mix():
        shape = (STATES, LON * STATES)
        to_row, c = row_values(shape, lon_decay)
        from_col = iota(shape, 1)
        same = (from_col % STATES) // 4 == to_row // 4
        spread = to_row % 4 - from_col % 4
        cells = ((from_col // STATES) * COLS).astype(F32)
        closing = jnp.exp(-cells * c)
        t = [closing * rising(cells - 1.0, k) for k in range(4)]
        circle = jnp.full(shape, float(COLS * LON), F32)
        closed = jnp.exp(-circle * c)
        n = [closed * rising(circle - 1.0, k) for k in range(4)]
        p = [1.0 / (1.0 - n[0])]
        p.append(p[0] * (n[1] * p[0]))
        p.append(p[0] * (n[1] * p[1] + n[2] * p[0]))
        p.append(p[0] * (n[1] * p[2] + n[2] * p[1] + n[3] * p[0]))
        m = [sum(t[j] * p[k - j] for j in range(k + 1)) for k in range(4)]
        mix = jnp.zeros(shape, F32)
        for k in range(4):
            mix = jnp.where(same & (spread == k), m[k], mix)
        mix_hi[...], mix_lo[...] = halves(mix)

    def lon_incoming(phase, g):
        for delta in range(1, LON):
            lon_copy(phase, g, delta).wait_recv()
        mix = (mix_hi[...], mix_lo[...])
        incoming = dot3(mix, halves(lon_slots[phase][g][...]), ((1,), (0,)))
        lon_in[g][...] = jnp.transpose(incoming)

    def enter(y, ent, g):
        weights = jnp.where(row // 4 == y, ent[...], 0.0)
        return dot3(halves(lon_in[g][...]), halves(weights), ((1,), (0,)))

    lon_mix()
    load_d.wait()

    def d_plane(y, first=0, count=FIELDS):
        return dvm[pl.ds(first * ROWS + y, count, stride=ROWS), :]

    lon_states(d_plane, fin_f, 0, 0)
    lon_states(d_plane, fin_f, 0, 1)
    pl.semaphore_wait(barrier, LON - 1 + 2 + MEM - 1)
    for g in range(2):
        for delta in range(1, LON):
            lon_copy(0, g, delta).start()

    def inside_f(y, carry):
        planes[y] = dot3(halves(d_plane(y)), (kf_hi[y], kf_lo[y]), ((1,), (0,)))
        return carry

    lax.fori_loop(0, ROWS, inside_f, 0)

    def entered_f(g):
        lon_incoming(0, g)
        at = pl.ds(*GROUPS[g])
        for y in range(ROWS):
            planes[y, at, :] = planes[y, at, :] + enter(y, ent_f, g)

    OWN, AHEAD_IN, TOTAL_IN, AHEAD_OUT, TOTAL_OUT = range(5)

    def lat_copy(bufs, phase, c, source, ahead, step):
        sign = step if phase == 0 else -step
        stream = 0 if ahead else 1
        return pltpu.make_async_remote_copy(
            src_ref=bufs.at[source, c],
            dst_ref=bufs.at[AHEAD_IN if ahead else TOTAL_IN, c],
            send_sem=lat_s.at[phase, stream, c],
            recv_sem=lat_r.at[phase, stream, c],
            device_id={"lat": lax.rem(me_lat + (LAT + sign), LAT)},
            device_id_type=MESH,
        )

    def advance(v, f):
        v1 = q * v[0] + f
        v2 = q * v[1] + v1
        v3 = q * v[2] + v2
        v4 = q * v[3] + v3
        return [v1, v2, v3, v4]

    def own_states(get_row, order, bufs, c):
        v = [jnp.zeros((CHUNK, COLS), F32)] * 4
        for y in order:
            v = advance(v, get_row(y))
        for s in range(4):
            bufs[OWN, c, s] = v[s]

    def transition(cells):
        closing = jnp.exp(-cells * c_lat)
        offset = jnp.zeros((1, COLS), F32) + (cells - 1.0)
        return [jnp.broadcast_to(closing * rising(offset, k), (CHUNK, COLS)) for k in range(4)]

    one_block = transition(float(ROWS))

    def add_moved(move, moved, fixed, result, bufs, c):
        v = [bufs[moved, c, s] for s in range(4)]
        w = [bufs[fixed, c, s] for s in range(4)]
        for s in range(4):
            total = w[s]
            for j in range(s + 1):
                total = total + move[s - j] * v[j]
            bufs[result, c, s] = total

    def is_in(p, *places):
        return functools.reduce(jnp.logical_or, [p == k for k in places])

    def places_of(phase):
        p = me_lat if phase == 0 else LAT - 1 - me_lat
        blocks = jnp.where(p < 4, 3 - p, p - 4)
        return p, transition((blocks * ROWS).astype(F32))

    def lat_begin(bufs, phase, p, c):
        @pl.when(is_in(p, 0, 4))
        def _():
            lat_copy(bufs, phase, c, OWN, True, 1).start()

        @pl.when(p == 3)
        def _():
            lat_copy(bufs, phase, c, OWN, False, -1).start()

        @pl.when(p == 0)
        def _():
            bufs[AHEAD_IN, c] = jnp.zeros((4, CHUNK, COLS), F32)

    def lat_streams(bufs, phase, p, far, prepare=None):
        wait_all = 0 if prepare is None else CHUNKS
        late_ahead = jnp.where(p == 2, LAG, jnp.where(p == 3, wait_all, 0))
        late_total = jnp.where(p == 1, LAG, jnp.where(p == 0, wait_all, 0))

        def chunk_of(t):
            return lax.rem(t + (FIRST if phase == 0 else 0) + CHUNKS, CHUNKS)

        def step(t, carry):
            a_at, b_at = t - late_ahead, t - late_total
            a, b = chunk_of(a_at), chunk_of(b_at)
            if prepare is not None:

                @pl.when((lax.rem(t, GROUP) == 0) & (t < CHUNKS))
                def _():
                    prepare(t // GROUP)


            @pl.when(is_in(p, 1, 2, 3, 5, 6) & (a_at >= 0) & (a_at < CHUNKS))
            def _():
                lat_copy(bufs, phase, a, AHEAD_OUT, True, 1).wait_recv()
                add_moved(one_block, AHEAD_IN, OWN, AHEAD_OUT, bufs, a)
                lat_copy(bufs, phase, a, AHEAD_OUT, True, 1).start()

            @pl.when((p < 3) & (b_at >= 0) & (b_at < CHUNKS))
            def _():
                lat_copy(bufs, phase, b, TOTAL_OUT, False, -1).wait_recv()
                add_moved(far, OWN, TOTAL_IN, TOTAL_OUT, bufs, b)
                lat_copy(bufs, phase, b, TOTAL_OUT, False, -1).start()

            return carry

        lax.fori_loop(0, CHUNKS + max(LAG, wait_all), step, 0)

    def lat_finish(bufs, phase, p, far, c):
        @pl.when(is_in(p, 4, 7))
        def _():
            lat_copy(bufs, phase, c, AHEAD_OUT, True, 1).wait_recv()

        @pl.when(p == 4)
        def _():
            lat_copy(bufs, phase, c, AHEAD_IN, False, 1).start()

        @pl.when(p > 4)
        def _():
            lat_copy(bufs, phase, c, TOTAL_OUT, False, -1).wait_recv()

        @pl.when(p == 7)
        def _():
            lat_copy(bufs, phase, c, TOTAL_IN, False, -1).start()

        @pl.when(p > 4)
        def _():
            add_moved(far, TOTAL_IN, AHEAD_IN, AHEAD_IN, bufs, c)

        return [bufs[AHEAD_IN, c, s] for s in range(4)]

    def lat_left(bufs, phase, p):
        def left(c, carry):
            @pl.when(p < 7)
            def _():
                lat_copy(bufs, phase, c, AHEAD_OUT, True, 1).wait_send()

            @pl.when((p < 5) | (p == 7))
            def _():
                lat_copy(bufs, phase, c, TOTAL_OUT, False, -1).wait_send()

            return carry

        lax.fori_loop(0, CHUNKS, left, 0)

    p_f, far_f = places_of(0)
    p_b, far_b = places_of(1)

    def fields_of(c):
        return pl.ds(pl.multiple_of(c * CHUNK, CHUNK), CHUNK)

    def start_f(c, carry):
        own_states(lambda y: planes[y, fields_of(c), :], range(ROWS), lat_f, c)
        lat_begin(lat_f, 0, p_f, c)
        return carry

    entered_f(0)
    lax.fori_loop(FIRST, CHUNKS, start_f, 0)
    entered_f(1)
    lax.fori_loop(0, FIRST, start_f, 0)

    for e in range(MODES):
        for l in range(LEVELS):
            vtab[l * MODES + e] = jnp.full((8, COLS), vert_modes[e, l], F32)
    lax.fori_loop(0, ROWS, tables_b, 0)
    load_m.wait()
    minc[me_mem] = jnp.zeros((LEVELS * ROWS, COLS), F32)

    mode = iota((CHUNK, COLS), 0)

    def active(c):
        return jnp.where(mode < eig_count[c], 1.0, 0.0)

    lat_streams(lat_f, 0, p_f, far_f)

    def chain_f(turn, carry):
        g = lax.rem(turn + FIRST // GROUP, CHUNKS // GROUP)
        w = []
        for k in range(GROUP):
            c = g * GROUP + k
            v = lat_finish(lat_f, 0, p_f, far_f, c)
            scale = gain_lat * active(c)
            for y in range(ROWS):
                v = advance(v, planes[y, fields_of(c), :])
                nat[pl.ds(c * (CHUNK * ROWS) + y, CHUNK, stride=ROWS), :] = v[3] * scale
            base = pl.multiple_of(c * (CHUNK * ROWS), CHUNK * ROWS)
            w.append([nat[pl.ds(base + e * ROWS, ROWS), :] for e in range(MODES)])

        def levels(pair, carry):
            at = pl.ds(pl.multiple_of(pair * 16, 16), 16)
            ens = [mvm[g * GROUP + m, at, :].astype(F32) for m in range(GROUP)]
            for h in range(2):
                total = None
                for m in range(GROUP):
                    profile = None
                    for e in range(MODES):
                        term = vtab[(pair * 2 + h) * MODES + e] * w[m][e]
                        profile = term if profile is None else profile + term
                    term = ens[m][h * 8 : h * 8 + 8] * profile
                    total = term if total is None else total + term
                at = pl.ds(pl.multiple_of(pair * 16 + h * 8, 8), 8)
                minc[me_mem, at, :] = minc[me_mem, at, :] + total
            return carry

        lax.fori_loop(0, LEVELS // 2, levels, 0)
        return carry

    lax.fori_loop(0, CHUNKS // GROUP, chain_f, 0)

    def mem_copy(delta):
        return pltpu.make_async_remote_copy(
            src_ref=minc.at[me_mem],
            dst_ref=minc.at[me_mem],
            send_sem=mem_s.at[delta - 1],
            recv_sem=mem_r.at[delta - 1],
            device_id={"mem": lax.rem(me_mem + delta, MEM)},
            device_id_type=MESH,
        )

    for delta in range(1, MEM):
        mem_copy(delta).start()
    load_o.wait()
    for delta in range(1, MEM):
        mem_copy(delta).wait_recv()
    weighted[...] = ovm[...] * ((minc[0] + minc[1]) + (minc[2] + minc[3]))

    def start_b(g):
        def levels(pair, total):
            total = list(total)
            at = pl.ds(pl.multiple_of(pair * 16, 16), 16)
            weight = weighted[at, :]
            for m in range(GROUP):
                both = mvm[g * GROUP + m, at, :].astype(F32) * weight
                for h in range(2):
                    for e in range(MODES):
                        total[m * MODES + e] = (
                            total[m * MODES + e]
                            + vtab[(pair * 2 + h) * MODES + e] * both[h * 8 : h * 8 + 8]
                        )
            return tuple(total)

        zero = jnp.zeros((8, COLS), F32)
        total = lax.fori_loop(0, LEVELS // 2, levels, (zero,) * (GROUP * MODES))
        for k in range(GROUP):
            c = g * GROUP + k
            base = pl.multiple_of(c * (CHUNK * ROWS), CHUNK * ROWS)
            for e in range(MODES):
                nat[pl.ds(base + e * ROWS, ROWS), :] = total[k * MODES + e]
            mask = active(c)
            for y in range(ROWS):
                planes[y, fields_of(c), :] = (
                    nat[pl.ds(c * (CHUNK * ROWS) + y, CHUNK, stride=ROWS), :] * mask
                )
            own_states(lambda y: planes[y, fields_of(c), :], range(ROWS - 1, -1, -1), lat_b, c)
            lat_begin(lat_b, 1, p_b, c)

    lat_streams(lat_b, 1, p_b, far_b, start_b)

    def chain_b(c, carry):
        v = lat_finish(lat_b, 1, p_b, far_b, c)
        for y in range(ROWS - 1, -1, -1):
            v = advance(v, planes[y, fields_of(c), :])
            planes[y, fields_of(c), :] = v[3] * gain_lat
        return carry

    def z_plane(y, first, count):
        return planes[y, pl.ds(first, count), :]

    lax.fori_loop(0, FIRST, chain_b, 0)
    lon_states(z_plane, fin_b, 1, 1)
    for delta in range(1, LON):
        lon_copy(1, 1, delta).start()
    lax.fori_loop(FIRST, CHUNKS, chain_b, 0)
    lon_states(z_plane, fin_b, 1, 0)
    for delta in range(1, LON):
        lon_copy(1, 0, delta).start()

    def inside_b(y, carry):
        planes[y] = dot3(halves(planes[y]), (kb_hi[y], kb_lo[y]), ((1,), (0,)))
        return carry

    lax.fori_loop(0, ROWS, inside_b, 0)
    load_r.wait()
    sums = [jnp.zeros((8, COLS), F32)] * 4
    stores = []
    for g in (1, 0):
        first, count = GROUPS[g]
        lon_incoming(1, g)
        for y in range(ROWS):
            at = pl.ds(first * ROWS + y, count, stride=ROWS)
            d, r = dvm[at, :], rvm[at, :]
            h = d + (z_plane(y, first, count) + enter(y, ent_b, g))
            nat[at, :] = h
            for k, product in enumerate((r * r, d * h, r * h, h * h)):
                sums[k] = sums[k] + jnp.sum(product.reshape(count // 8, 8, COLS), axis=0)
        part = pl.ds(first * ROWS, count * ROWS)
        stores.append(pltpu.make_async_copy(nat.at[part], hess_out.at[part], out_sem.at[g]))
        stores[-1].start()

    for k in range(4):
        tile[pl.ds(k, 1), :] = jnp.sum(sums[k], axis=0, keepdims=True)
    tile[pl.ds(4, 4), :] = jnp.zeros((4, COLS), F32)

    def reduce(slots, me, s_sem, r_sem, peers):
        slots[me] = tile[...]

        def copies():
            for k, peer in enumerate(peers):
                yield pltpu.make_async_remote_copy(
                    src_ref=slots.at[me],
                    dst_ref=slots.at[me],
                    send_sem=s_sem.at[k],
                    recv_sem=r_sem.at[k],
                    device_id=peer,
                    device_id_type=MESH,
                )

        for copy in copies():
            copy.start()
        for copy in copies():
            copy.wait_recv()
        total = slots[0]
        for k in range(1, len(peers) + 1):
            total = total + slots[k]
        tile[...] = total
        return copies

    left_a = reduce(
        red_a, me_mem * LON + me_lon, ra_s, ra_r,
        [
            {"lon": lax.rem(me_lon + dx, LON), "mem": lax.rem(me_mem + dy, MEM)}
            for dy in range(MEM) for dx in range(LON) if dx or dy
        ],
    )
    left_c = reduce(
        red_c, me_lat, rc_s, rc_r, [{"lat": lax.rem(me_lat + dz, LAT)} for dz in range(1, LAT)]
    )
    sums = jnp.broadcast_to(jnp.sum(tile[...], axis=1, keepdims=True), (8, COLS))
    rr, dh, rh, hh = (sums[k : k + 1] for k in range(4))
    step = rr / dh
    norm_new = rr - 2.0 * step * rh + step * step * hh
    step_out[0, 0] = step[0, 0]
    ratio_out[0, 0] = (norm_new / rr)[0, 0]

    for store in stores:
        store.wait()
    for phase in range(2):
        for g in range(2):
            for delta in range(1, LON):
                lon_copy(phase, g, delta).wait_send()
    for delta in range(1, MEM):
        mem_copy(delta).wait_send()
    for left in (left_a, left_c):
        for copy in left():
            copy.wait_send()
    lat_left(lat_f, 0, p_f)
    lat_left(lat_b, 1, p_b)


def body(control, residual, direction, members, vert_modes, eig_count, lon_decay, lat_decay, obs_weight):
    rows = FIELDS * ROWS
    any_space = pl.BlockSpec(memory_space=pl.ANY)
    smem = pl.BlockSpec(memory_space=pltpu.SMEM)
    dma = pltpu.SemaphoreType.DMA
    states = pltpu.VMEM((5, CHUNKS, 4, CHUNK, COLS), F32)
    table = pltpu.VMEM((ROWS, COLS, COLS), BF16)
    slots = [pltpu.VMEM((LON * STATES, count), F32) for first, count in GROUPS]
    mix = pltpu.VMEM((STATES, LON * STATES), BF16)
    small = pltpu.VMEM((STATES, COLS), F32)
    one = jax.ShapeDtypeStruct((1, 1), F32)
    hessian, step, ratio = pl.pallas_call(
        kernel,
        name="cg_step",
        out_shape=(
            jax.ShapeDtypeStruct((rows, COLS), F32),
            one, one,
        ),
        in_specs=[any_space] * 8,
        out_specs=(any_space, smem, smem),
        scratch_shapes=[
            pltpu.SMEM(vert_modes.shape, F32),
            pltpu.SMEM(eig_count.shape, jnp.int32),
            pltpu.SMEM(lon_decay.shape, F32),
            pltpu.VMEM((1, COLS), F32),
            pltpu.VMEM((rows, COLS), F32),
            pltpu.VMEM((rows, COLS), F32),
            pltpu.VMEM((FIELDS // MODES, LEVELS * ROWS, COLS), BF16),
            pltpu.VMEM((LEVELS * ROWS, COLS), F32),
            pltpu.VMEM((rows, COLS), F32),
            pltpu.VMEM((ROWS, FIELDS, COLS), F32),
            table, table, table, table,
            pltpu.VMEM((LEVELS * MODES, 8, COLS), F32),
            *slots, *slots,
            *[pltpu.VMEM((count, STATES), F32) for first, count in GROUPS],
            mix, mix,
            small, small, small, small,
            states, states,
            pltpu.VMEM((MEM, LEVELS * ROWS, COLS), F32),
            pltpu.VMEM((LEVELS * ROWS, COLS), F32),
            pltpu.VMEM((LON * MEM, 8, COLS), F32),
            pltpu.VMEM((LAT, 8, COLS), F32),
            pltpu.VMEM((8, COLS), F32),
            dma((8,)), dma((2,)),
            dma((2, 2, LON - 1)), dma((2, 2, LON - 1)),
            dma((2, 2, CHUNKS)), dma((2, 2, CHUNKS)),
            dma((MEM - 1,)), dma((MEM - 1,)),
            dma((LON * MEM - 1,)), dma((LON * MEM - 1,)),
            dma((LAT - 1,)), dma((LAT - 1,)),
        ],
        compiler_params=pltpu.CompilerParams(
            collective_id=0, has_side_effects=True, vmem_limit_bytes=60 << 20
        ),
    )(
        direction.reshape(rows, COLS),
        residual.reshape(rows, COLS),
        members.reshape(FIELDS // MODES, LEVELS * ROWS, COLS),
        vert_modes,
        eig_count,
        lon_decay,
        lat_decay.reshape(1, COLS),
        obs_weight.reshape(LEVELS * ROWS, COLS),
    )
    hessian = hessian.reshape(direction.shape)
    step, ratio = step.reshape(()), ratio.reshape(())
    new_control = control + step * direction
    new_residual = residual - step * hessian
    new_direction = new_residual + ratio * direction
    return new_control, new_residual, new_direction


def solution(mesh):
    field = P("mem", "lat", "lon")
    placed = (
        field, field, field, P("mem", None, "lat", "lon"), P(), P("mem"), P("lat"), P("lon"),
        P(None, "lat", "lon"),
    )
    return jax.shard_map(
        body, mesh=mesh, in_specs=placed, out_specs=(field, field, field), check_vma=False
    )
```

```python
import functools

import jax
import jax.numpy as jnp
from jax import lax
from jax.experimental import pallas as pl
from jax.experimental.pallas import tpu as pltpu
from jax.sharding import PartitionSpec as P

MESH = pl.DeviceIdType.MESH
F32 = jnp.float32
BF16 = jnp.bfloat16

LON, LAT, MEM = 8, 8, 4
FIELDS, ROWS, COLS = 160, 8, 128
LEVELS, MODES = 32, 8
CHUNK = 8
GROUP = 2
LAG = 10
CHUNKS = FIELDS // CHUNK
GROUPS = ((128, 32), (0, 128))
FIRST = 16
STATES = 4 * ROWS


def leak(c):
    series = jnp.ones_like(c)
    for k in range(10, 1, -1):
        series = 1.0 - (c / float(k)) * series
    return c * series


def rising(offset, degree):
    result = jnp.ones_like(offset)
    for k in range(degree):
        result = result * (offset + (k + 1.0)) * (1.0 / (k + 1.0))
    return result


def halves(x):
    high = x.astype(BF16)
    return high, (x - high.astype(F32)).astype(BF16)


def dot3(a, b, dims):
    dot = functools.partial(lax.dot_general, dimension_numbers=(dims, ((), ())), preferred_element_type=F32)
    return dot(a[0], b[0]) + (dot(a[0], b[1]) + dot(a[1], b[0]))


def far_first(count):
    return sorted(range(1, count), key=lambda d: -min(d, count - d))


def iota(shape, dim):
    return lax.broadcasted_iota(jnp.int32, shape, dim)


def row_values(shape, lon_decay):
    row = iota(shape, 0)
    c = jnp.zeros(shape, F32)
    for y in range(ROWS):
        c = jnp.where(row // 4 == y, lon_decay[y], c)
    return row, c


def lon_gain(c):
    a = leak(c)
    return a * a * a * jnp.sqrt(a) * 2.5


def kernel(
    direction, residual, members, vert_modes_in, eig_count_in, lon_decay_in, lat_decay_in, obs_weight,
    hess_out, step_out, ratio_out,
    vert_modes, eig_count, lon_decay, lat_decay, dvm, rvm, mvm, ovm, nat, planes, kf_hi, kf_lo, kb_hi, kb_lo, vtab,
    lon_fa, lon_fb, lon_ba, lon_bb, in_a, in_b, mix_hi, mix_lo, fin_f, fin_b, ent_f, ent_b,
    lat_f, lat_b, minc, weighted, red_a, red_c, tile,
    in_sem, out_sem, lon_s, lon_r, lat_s, lat_r, mem_s, mem_r, ra_s, ra_r, rc_s, rc_r,
):
    me_lon, me_lat, me_mem = lax.axis_index("lon"), lax.axis_index("lat"), lax.axis_index("mem")

    barrier = pltpu.get_barrier_semaphore()
    for axis, me, count in (("lon", me_lon, LON), ("lat", me_lat, LAT), ("mem", me_mem, MEM)):
        for delta in (1, LAT - 1) if axis == "lat" else far_first(count):
            pl.semaphore_signal(
                barrier, inc=1, device_id={axis: lax.rem(me + delta, count)}, device_id_type=MESH
            )

    load_d = pltpu.make_async_copy(direction, dvm, in_sem.at[0])
    load_m = pltpu.make_async_copy(members, mvm, in_sem.at[1])
    load_o = pltpu.make_async_copy(obs_weight, ovm, in_sem.at[2])
    load_r = pltpu.make_async_copy(residual, rvm, in_sem.at[3])
    small = [
        pltpu.make_async_copy(lon_decay_in, lon_decay, in_sem.at[4]),
        pltpu.make_async_copy(lat_decay_in, lat_decay, in_sem.at[5]),
        pltpu.make_async_copy(vert_modes_in, vert_modes, in_sem.at[6]),
        pltpu.make_async_copy(eig_count_in, eig_count, in_sem.at[7]),
    ]
    for load in (*small, load_d, load_m, load_o, load_r):
        load.start()
    for load in small:
        load.wait()

    row, c_row = row_values((STATES, COLS), lon_decay)
    section = row % 4
    column = iota((STATES, COLS), 1).astype(F32)

    def pick(entries):
        result = entries[3]
        for s in range(3):
            result = jnp.where(section == s, entries[s], result)
        return result

    gain_row = lon_gain(c_row)
    last = COLS - 1.0
    fin_f[...] = pick([rising(last - column, s) for s in range(4)]) * jnp.exp(-(last - column) * c_row)
    fin_b[...] = pick([rising(column, s) for s in range(4)]) * jnp.exp(-column * c_row)
    ent_f[...] = (
        gain_row * pick([rising(column, 3 - s) for s in range(4)]) * jnp.exp(-(column + 1.0) * c_row)
    )
    ent_b[...] = (
        gain_row
        * pick([rising(last - column, 3 - s) for s in range(4)])
        * jnp.exp(-(last - column + 1.0) * c_row)
    )

    source = iota((COLS, COLS), 0)
    target = iota((COLS, COLS), 1)

    def response(offset, y):
        lag = jnp.maximum(offset, 0).astype(F32)
        c = jnp.full((COLS, COLS), lon_decay[y], F32)
        gain = lon_gain(jnp.full((8, COLS), lon_decay[y], F32))[0:1]
        return jnp.where(offset >= 0, rising(lag, 3) * gain * jnp.exp(-lag * c), 0.0)

    def tables_f(y, carry):
        kf_hi[y], kf_lo[y] = halves(response(target - source, y))
        return carry

    def tables_b(y, carry):
        kb_hi[y], kb_lo[y] = halves(response(source - target, y))
        return carry

    lax.fori_loop(0, ROWS, tables_f, 0)

    c_lat = lat_decay[...]
    q = jnp.broadcast_to(jnp.exp(-c_lat), (CHUNK, COLS))
    a_lat = leak(c_lat)
    gain_lat = jnp.broadcast_to(a_lat * a_lat * a_lat * jnp.sqrt(a_lat) * 2.5, (CHUNK, COLS))

    lon_slots = ((lon_fa, lon_fb), (lon_ba, lon_bb))
    lon_in = (in_a, in_b)

    def lon_states(get_plane, fin, phase, g):
        first, count = GROUPS[g]
        total = jnp.zeros((STATES, count), F32)
        for y in range(ROWS):
            weights = jnp.where(row // 4 == y, fin[...], 0.0)
            total = total + dot3(halves(weights), halves(get_plane(y, first, count)), ((1,), (1,)))
        lon_slots[phase][g][pl.ds((LON - 1) * STATES, STATES), :] = total

    def lon_copy(phase, g, delta):
        sign = 1 if phase == 0 else LON - 1
        slots = lon_slots[phase][g]
        return pltpu.make_async_remote_copy(
            src_ref=slots.at[pl.ds((LON - 1) * STATES, STATES)],
            dst_ref=slots.at[pl.ds((delta - 1) * STATES, STATES)],
            send_sem=lon_s.at[phase, g, delta - 1],
            recv_sem=lon_r.at[phase, g, delta - 1],
            device_id={"lon": lax.rem(me_lon + sign * delta, LON)},
            device_id_type=MESH,
        )

    def lon_mix():
        shape = (STATES, LON * STATES)
        to_row, c = row_values(shape, lon_decay)
        from_col = iota(shape, 1)
        same = (from_col % STATES) // 4 == to_row // 4
        spread = to_row % 4 - from_col % 4
        cells = ((from_col // STATES) * COLS).astype(F32)
        closing = jnp.exp(-cells * c)
        t = [closing * rising(cells - 1.0, k) for k in range(4)]
        circle = jnp.full(shape, float(COLS * LON), F32)
        closed = jnp.exp(-circle * c)
        n = [closed * rising(circle - 1.0, k) for k in range(4)]
        p = [1.0 / (1.0 - n[0])]
        p.append(p[0] * (n[1] * p[0]))
        p.append(p[0] * (n[1] * p[1] + n[2] * p[0]))
        p.append(p[0] * (n[1] * p[2] + n[2] * p[1] + n[3] * p[0]))
        m = [sum(t[j] * p[k - j] for j in range(k + 1)) for k in range(4)]
        mix = jnp.zeros(shape, F32)
        for k in range(4):
            mix = jnp.where(same & (spread == k), m[k], mix)
        mix_hi[...], mix_lo[...] = halves(mix)

    def lon_incoming(phase, g):
        for delta in range(1, LON):
            lon_copy(phase, g, delta).wait_recv()
        mix = (mix_hi[...], mix_lo[...])
        incoming = dot3(mix, halves(lon_slots[phase][g][...]), ((1,), (0,)))
        lon_in[g][...] = jnp.transpose(incoming)

    def enter(y, ent, g):
        weights = jnp.where(row // 4 == y, ent[...], 0.0)
        return dot3(halves(lon_in[g][...]), halves(weights), ((1,), (0,)))

    lon_mix()
    load_d.wait()

    def d_plane(y, first=0, count=FIELDS):
        return dvm[pl.ds(first * ROWS + y, count, stride=ROWS), :]

    lon_states(d_plane, fin_f, 0, 0)
    lon_states(d_plane, fin_f, 0, 1)
    pl.semaphore_wait(barrier, LON - 1 + 2 + MEM - 1)
    for g in range(2):
        for delta in far_first(LON):
            lon_copy(0, g, delta).start()

    def inside_f(y, carry):
        planes[y] = dot3(halves(d_plane(y)), (kf_hi[y], kf_lo[y]), ((1,), (0,)))
        return carry

    lax.fori_loop(0, ROWS, inside_f, 0)

    def entered_f(g):
        lon_incoming(0, g)
        at = pl.ds(*GROUPS[g])
        for y in range(ROWS):
            planes[y, at, :] = planes[y, at, :] + enter(y, ent_f, g)

    OWN, AHEAD_IN, TOTAL_IN, AHEAD_OUT, TOTAL_OUT = range(5)

    def lat_copy(bufs, phase, c, source, ahead, step):
        sign = step if phase == 0 else -step
        stream = 0 if ahead else 1
        return pltpu.make_async_remote_copy(
            src_ref=bufs.at[source, c],
            dst_ref=bufs.at[AHEAD_IN if ahead else TOTAL_IN, c],
            send_sem=lat_s.at[phase, stream, c],
            recv_sem=lat_r.at[phase, stream, c],
            device_id={"lat": lax.rem(me_lat + (LAT + sign), LAT)},
            device_id_type=MESH,
        )

    def advance(v, f):
        v1 = q * v[0] + f
        v2 = q * v[1] + v1
        v3 = q * v[2] + v2
        v4 = q * v[3] + v3
        return [v1, v2, v3, v4]

    def own_states(get_row, order, bufs, c):
        v = [jnp.zeros((CHUNK, COLS), F32)] * 4
        for y in order:
            v = advance(v, get_row(y))
        for s in range(4):
            bufs[OWN, c, s] = v[s]

    def transition(cells):
        closing = jnp.exp(-cells * c_lat)
        offset = jnp.zeros((1, COLS), F32) + (cells - 1.0)
        return [jnp.broadcast_to(closing * rising(offset, k), (CHUNK, COLS)) for k in range(4)]

    one_block = transition(float(ROWS))

    def add_moved(move, moved, fixed, result, bufs, c):
        v = [bufs[moved, c, s] for s in range(4)]
        w = [bufs[fixed, c, s] for s in range(4)]
        for s in range(4):
            total = w[s]
            for j in range(s + 1):
                total = total + move[s - j] * v[j]
            bufs[result, c, s] = total

    def is_in(p, *places):
        return functools.reduce(jnp.logical_or, [p == k for k in places])

    def places_of(phase):
        p = me_lat if phase == 0 else LAT - 1 - me_lat
        blocks = jnp.where(p < 4, 3 - p, p - 4)
        return p, transition((blocks * ROWS).astype(F32))

    def lat_begin(bufs, phase, p, c):
        @pl.when(is_in(p, 0, 4))
        def _():
            lat_copy(bufs, phase, c, OWN, True, 1).start()

        @pl.when(p == 3)
        def _():
            lat_copy(bufs, phase, c, OWN, False, -1).start()

        @pl.when(p == 0)
        def _():
            bufs[AHEAD_IN, c] = jnp.zeros((4, CHUNK, COLS), F32)

    def lat_streams(bufs, phase, p, far, prepare=None):
        wait_all = 0 if prepare is None else CHUNKS
        late_ahead = jnp.where(p == 2, LAG, jnp.where(p == 3, wait_all, 0))
        late_total = jnp.where(p == 1, LAG, jnp.where(p == 0, wait_all, 0))

        def chunk_of(t):
            return lax.rem(t + (FIRST if phase == 0 else 0) + CHUNKS, CHUNKS)

        def step(t, carry):
            a_at, b_at = t - late_ahead, t - late_total
            a, b = chunk_of(a_at), chunk_of(b_at)
            if prepare is not None:

                @pl.when((lax.rem(t, GROUP) == 0) & (t < CHUNKS))
                def _():
                    prepare(t // GROUP)


            @pl.when(is_in(p, 1, 2, 3, 5, 6) & (a_at >= 0) & (a_at < CHUNKS))
            def _():
                lat_copy(bufs, phase, a, AHEAD_OUT, True, 1).wait_recv()
                add_moved(one_block, AHEAD_IN, OWN, AHEAD_OUT, bufs, a)
                lat_copy(bufs, phase, a, AHEAD_OUT, True, 1).start()

            @pl.when((p < 3) & (b_at >= 0) & (b_at < CHUNKS))
            def _():
                lat_copy(bufs, phase, b, TOTAL_OUT, False, -1).wait_recv()
                add_moved(far, OWN, TOTAL_IN, TOTAL_OUT, bufs, b)
                lat_copy(bufs, phase, b, TOTAL_OUT, False, -1).start()

            return carry

        lax.fori_loop(0, CHUNKS + max(LAG, wait_all), step, 0)

    def lat_finish(bufs, phase, p, far, c):
        @pl.when(is_in(p, 4, 7))
        def _():
            lat_copy(bufs, phase, c, AHEAD_OUT, True, 1).wait_recv()

        @pl.when(p == 4)
        def _():
            lat_copy(bufs, phase, c, AHEAD_IN, False, 1).start()

        @pl.when(p > 4)
        def _():
            lat_copy(bufs, phase, c, TOTAL_OUT, False, -1).wait_recv()

        @pl.when(p == 7)
        def _():
            lat_copy(bufs, phase, c, TOTAL_IN, False, -1).start()

        @pl.when(p > 4)
        def _():
            add_moved(far, TOTAL_IN, AHEAD_IN, AHEAD_IN, bufs, c)

        return [bufs[AHEAD_IN, c, s] for s in range(4)]

    def lat_left(bufs, phase, p):
        def left(c, carry):
            @pl.when(p < 7)
            def _():
                lat_copy(bufs, phase, c, AHEAD_OUT, True, 1).wait_send()

            @pl.when((p < 5) | (p == 7))
            def _():
                lat_copy(bufs, phase, c, TOTAL_OUT, False, -1).wait_send()

            return carry

        lax.fori_loop(0, CHUNKS, left, 0)

    p_f, far_f = places_of(0)
    p_b, far_b = places_of(1)

    def fields_of(c):
        return pl.ds(pl.multiple_of(c * CHUNK, CHUNK), CHUNK)

    def start_f(c, carry):
        own_states(lambda y: planes[y, fields_of(c), :], range(ROWS), lat_f, c)
        lat_begin(lat_f, 0, p_f, c)
        return carry

    entered_f(0)
    lax.fori_loop(FIRST, CHUNKS, start_f, 0)
    entered_f(1)
    lax.fori_loop(0, FIRST, start_f, 0)

    for e in range(MODES):
        for l in range(LEVELS):
            vtab[l * MODES + e] = jnp.full((8, COLS), vert_modes[e, l], F32)
    lax.fori_loop(0, ROWS, tables_b, 0)
    load_m.wait()
    minc[me_mem] = jnp.zeros((LEVELS * ROWS, COLS), F32)

    mode = iota((CHUNK, COLS), 0)

    def active(c):
        return jnp.where(mode < eig_count[c], 1.0, 0.0)

    lat_streams(lat_f, 0, p_f, far_f)

    def chain_f(turn, carry):
        g = lax.rem(turn + FIRST // GROUP, CHUNKS // GROUP)
        w = []
        for k in range(GROUP):
            c = g * GROUP + k
            v = lat_finish(lat_f, 0, p_f, far_f, c)
            scale = gain_lat * active(c)
            for y in range(ROWS):
                v = advance(v, planes[y, fields_of(c), :])
                nat[pl.ds(c * (CHUNK * ROWS) + y, CHUNK, stride=ROWS), :] = v[3] * scale
            base = pl.multiple_of(c * (CHUNK * ROWS), CHUNK * ROWS)
            w.append([nat[pl.ds(base + e * ROWS, ROWS), :] for e in range(MODES)])

        def levels(pair, carry):
            at = pl.ds(pl.multiple_of(pair * 16, 16), 16)
            ens = [mvm[g * GROUP + m, at, :].astype(F32) for m in range(GROUP)]
            for h in range(2):
                total = None
                for m in range(GROUP):
                    profile = None
                    for e in range(MODES):
                        term = vtab[(pair * 2 + h) * MODES + e] * w[m][e]
                        profile = term if profile is None else profile + term
                    term = ens[m][h * 8 : h * 8 + 8] * profile
                    total = term if total is None else total + term
                at = pl.ds(pl.multiple_of(pair * 16 + h * 8, 8), 8)
                minc[me_mem, at, :] = minc[me_mem, at, :] + total
            return carry

        lax.fori_loop(0, LEVELS // 2, levels, 0)
        return carry

    lax.fori_loop(0, CHUNKS // GROUP, chain_f, 0)

    def mem_copy(delta):
        return pltpu.make_async_remote_copy(
            src_ref=minc.at[me_mem],
            dst_ref=minc.at[me_mem],
            send_sem=mem_s.at[delta - 1],
            recv_sem=mem_r.at[delta - 1],
            device_id={"mem": lax.rem(me_mem + delta, MEM)},
            device_id_type=MESH,
        )

    for delta in far_first(MEM):
        mem_copy(delta).start()
    load_o.wait()
    for delta in range(1, MEM):
        mem_copy(delta).wait_recv()
    weighted[...] = ovm[...] * ((minc[0] + minc[1]) + (minc[2] + minc[3]))

    def start_b(g):
        def levels(pair, total):
            total = list(total)
            at = pl.ds(pl.multiple_of(pair * 16, 16), 16)
            weight = weighted[at, :]
            for m in range(GROUP):
                both = mvm[g * GROUP + m, at, :].astype(F32) * weight
                for h in range(2):
                    for e in range(MODES):
                        total[m * MODES + e] = (
                            total[m * MODES + e]
                            + vtab[(pair * 2 + h) * MODES + e] * both[h * 8 : h * 8 + 8]
                        )
            return tuple(total)

        zero = jnp.zeros((8, COLS), F32)
        total = lax.fori_loop(0, LEVELS // 2, levels, (zero,) * (GROUP * MODES))
        for k in range(GROUP):
            c = g * GROUP + k
            base = pl.multiple_of(c * (CHUNK * ROWS), CHUNK * ROWS)
            for e in range(MODES):
                nat[pl.ds(base + e * ROWS, ROWS), :] = total[k * MODES + e]
            mask = active(c)
            for y in range(ROWS):
                planes[y, fields_of(c), :] = (
                    nat[pl.ds(c * (CHUNK * ROWS) + y, CHUNK, stride=ROWS), :] * mask
                )
            own_states(lambda y: planes[y, fields_of(c), :], range(ROWS - 1, -1, -1), lat_b, c)
            lat_begin(lat_b, 1, p_b, c)

    lat_streams(lat_b, 1, p_b, far_b, start_b)

    def chain_b(c, carry):
        v = lat_finish(lat_b, 1, p_b, far_b, c)
        for y in range(ROWS - 1, -1, -1):
            v = advance(v, planes[y, fields_of(c), :])
            planes[y, fields_of(c), :] = v[3] * gain_lat
        return carry

    def z_plane(y, first, count):
        return planes[y, pl.ds(first, count), :]

    lax.fori_loop(0, FIRST, chain_b, 0)
    lon_states(z_plane, fin_b, 1, 1)
    for delta in far_first(LON):
        lon_copy(1, 1, delta).start()
    lax.fori_loop(FIRST, CHUNKS, chain_b, 0)
    lon_states(z_plane, fin_b, 1, 0)
    for delta in far_first(LON):
        lon_copy(1, 0, delta).start()

    def inside_b(y, carry):
        planes[y] = dot3(halves(planes[y]), (kb_hi[y], kb_lo[y]), ((1,), (0,)))
        return carry

    lax.fori_loop(0, ROWS, inside_b, 0)
    load_r.wait()
    sums = [jnp.zeros((8, COLS), F32)] * 4
    stores = []
    for g in (1, 0):
        first, count = GROUPS[g]
        lon_incoming(1, g)
        for y in range(ROWS):
            at = pl.ds(first * ROWS + y, count, stride=ROWS)
            d, r = dvm[at, :], rvm[at, :]
            h = d + (z_plane(y, first, count) + enter(y, ent_b, g))
            nat[at, :] = h
            for k, product in enumerate((r * r, d * h, r * h, h * h)):
                sums[k] = sums[k] + jnp.sum(product.reshape(count // 8, 8, COLS), axis=0)
        part = pl.ds(first * ROWS, count * ROWS)
        stores.append(pltpu.make_async_copy(nat.at[part], hess_out.at[part], out_sem.at[g]))
        stores[-1].start()

    for k in range(4):
        tile[pl.ds(k, 1), :] = jnp.sum(sums[k], axis=0, keepdims=True)
    tile[pl.ds(4, 4), :] = jnp.zeros((4, COLS), F32)

    def reduce(slots, me, s_sem, r_sem, peers, meanwhile):
        slots[me] = tile[...]

        def copies():
            for k, peer in enumerate(peers):
                yield pltpu.make_async_remote_copy(
                    src_ref=slots.at[me],
                    dst_ref=slots.at[me],
                    send_sem=s_sem.at[k],
                    recv_sem=r_sem.at[k],
                    device_id=peer,
                    device_id_type=MESH,
                )

        for copy in copies():
            copy.start()
        meanwhile()
        for copy in copies():
            copy.wait_recv()
        total = slots[0]
        for k in range(1, len(peers) + 1):
            total = total + slots[k]
        tile[...] = total
        return copies

    def departed():
        for store in stores:
            store.wait()
        for phase in range(2):
            for g in range(2):
                for delta in range(1, LON):
                    lon_copy(phase, g, delta).wait_send()
        for delta in range(1, MEM):
            mem_copy(delta).wait_send()
        lat_left(lat_f, 0, p_f)
        lat_left(lat_b, 1, p_b)

    def departed_a():
        for copy in left_a():
            copy.wait_send()

    left_a = reduce(
        red_a, me_mem * LON + me_lon, ra_s, ra_r,
        [
            {"lon": lax.rem(me_lon + dx, LON), "mem": lax.rem(me_mem + dy, MEM)}
            for dx, dy in sorted(
                [(dx, dy) for dy in range(MEM) for dx in range(LON) if dx or dy],
                key=lambda d: -(min(d[1], MEM - d[1]) + min(d[0], LON - d[0]) / 2),
            )
        ],
        departed,
    )
    left_c = reduce(
        red_c, me_lat, rc_s, rc_r, [{"lat": lax.rem(me_lat + dz, LAT)} for dz in far_first(LAT)],
        departed_a,
    )
    sums = jnp.broadcast_to(jnp.sum(tile[...], axis=1, keepdims=True), (8, COLS))
    rr, dh, rh, hh = (sums[k : k + 1] for k in range(4))
    step = rr / dh
    norm_new = rr - 2.0 * step * rh + step * step * hh
    step_out[0, 0] = step[0, 0]
    ratio_out[0, 0] = (norm_new / rr)[0, 0]

    for copy in left_c():
        copy.wait_send()


def body(control, residual, direction, members, vert_modes, eig_count, lon_decay, lat_decay, obs_weight):
    rows = FIELDS * ROWS
    any_space = pl.BlockSpec(memory_space=pl.ANY)
    smem = pl.BlockSpec(memory_space=pltpu.SMEM)
    dma = pltpu.SemaphoreType.DMA
    states = pltpu.VMEM((5, CHUNKS, 4, CHUNK, COLS), F32)
    table = pltpu.VMEM((ROWS, COLS, COLS), BF16)
    slots = [pltpu.VMEM((LON * STATES, count), F32) for first, count in GROUPS]
    mix = pltpu.VMEM((STATES, LON * STATES), BF16)
    small = pltpu.VMEM((STATES, COLS), F32)
    one = jax.ShapeDtypeStruct((1, 1), F32)
    hessian, step, ratio = pl.pallas_call(
        kernel,
        name="cg_step",
        out_shape=(
            jax.ShapeDtypeStruct((rows, COLS), F32),
            one, one,
        ),
        in_specs=[any_space] * 8,
        out_specs=(any_space, smem, smem),
        scratch_shapes=[
            pltpu.SMEM(vert_modes.shape, F32),
            pltpu.SMEM(eig_count.shape, jnp.int32),
            pltpu.SMEM(lon_decay.shape, F32),
            pltpu.VMEM((1, COLS), F32),
            pltpu.VMEM((rows, COLS), F32),
            pltpu.VMEM((rows, COLS), F32),
            pltpu.VMEM((FIELDS // MODES, LEVELS * ROWS, COLS), BF16),
            pltpu.VMEM((LEVELS * ROWS, COLS), F32),
            pltpu.VMEM((rows, COLS), F32),
            pltpu.VMEM((ROWS, FIELDS, COLS), F32),
            table, table, table, table,
            pltpu.VMEM((LEVELS * MODES, 8, COLS), F32),
            *slots, *slots,
            *[pltpu.VMEM((count, STATES), F32) for first, count in GROUPS],
            mix, mix,
            small, small, small, small,
            states, states,
            pltpu.VMEM((MEM, LEVELS * ROWS, COLS), F32),
            pltpu.VMEM((LEVELS * ROWS, COLS), F32),
            pltpu.VMEM((LON * MEM, 8, COLS), F32),
            pltpu.VMEM((LAT, 8, COLS), F32),
            pltpu.VMEM((8, COLS), F32),
            dma((8,)), dma((2,)),
            dma((2, 2, LON - 1)), dma((2, 2, LON - 1)),
            dma((2, 2, CHUNKS)), dma((2, 2, CHUNKS)),
            dma((MEM - 1,)), dma((MEM - 1,)),
            dma((LON * MEM - 1,)), dma((LON * MEM - 1,)),
            dma((LAT - 1,)), dma((LAT - 1,)),
        ],
        compiler_params=pltpu.CompilerParams(
            collective_id=0, has_side_effects=True, vmem_limit_bytes=60 << 20
        ),
    )(
        direction.reshape(rows, COLS),
        residual.reshape(rows, COLS),
        members.reshape(FIELDS // MODES, LEVELS * ROWS, COLS),
        vert_modes,
        eig_count,
        lon_decay,
        lat_decay.reshape(1, COLS),
        obs_weight.reshape(LEVELS * ROWS, COLS),
    )
    hessian = hessian.reshape(direction.shape)
    step, ratio = step.reshape(()), ratio.reshape(())
    new_control = control + step * direction
    new_residual = residual - step * hessian
    new_direction = new_residual + ratio * direction
    return new_control, new_residual, new_direction


def solution(mesh):
    field = P("mem", "lat", "lon")
    placed = (
        field, field, field, P("mem", None, "lat", "lon"), P(), P("mem"), P("lat"), P("lon"),
        P(None, "lat", "lon"),
    )
    return jax.shard_map(
        body, mesh=mesh, in_specs=placed, out_specs=(field, field, field), check_vma=False
    )
```

```python
import functools

import jax
import jax.numpy as jnp
from jax import lax
from jax.experimental import pallas as pl
from jax.experimental.pallas import tpu as pltpu
from jax.sharding import PartitionSpec as P

MESH = pl.DeviceIdType.MESH
F32 = jnp.float32
BF16 = jnp.bfloat16

LON, LAT, MEM = 8, 8, 4
FIELDS, ROWS, COLS = 160, 8, 128
LEVELS, MODES = 32, 8
CHUNK = 8
GROUP = 2
LAG = 9
CHUNKS = FIELDS // CHUNK
GROUPS = ((128, 32), (0, 128))
FIRST = 16
STATES = 4 * ROWS


def leak(c):
    series = jnp.ones_like(c)
    for k in range(10, 1, -1):
        series = 1.0 - (c / float(k)) * series
    return c * series


def rising(offset, degree):
    result = jnp.ones_like(offset)
    for k in range(degree):
        result = result * (offset + (k + 1.0)) * (1.0 / (k + 1.0))
    return result


def halves(x):
    high = x.astype(BF16)
    return high, (x - high.astype(F32)).astype(BF16)


def dot3(a, b, dims):
    dot = functools.partial(lax.dot_general, dimension_numbers=(dims, ((), ())), preferred_element_type=F32)
    return dot(a[0], b[0]) + (dot(a[0], b[1]) + dot(a[1], b[0]))


def far_first(count):
    return sorted(range(1, count), key=lambda d: -min(d, count - d))


def iota(shape, dim):
    return lax.broadcasted_iota(jnp.int32, shape, dim)


def row_values(shape, lon_decay):
    row = iota(shape, 0)
    c = jnp.zeros(shape, F32)
    for y in range(ROWS):
        c = jnp.where(row // 4 == y, lon_decay[y], c)
    return row, c


def lon_gain(c):
    a = leak(c)
    return a * a * a * jnp.sqrt(a) * 2.5


def kernel(
    direction, residual, members, vert_modes_in, eig_count_in, lon_decay_in, lat_decay_in, obs_weight,
    hess_out, step_out, ratio_out,
    vert_modes, eig_count, lon_decay, lat_decay, dvm, rvm, mvm, ovm, nat, planes, kf_hi, kf_lo, kb_hi, kb_lo, vtab,
    lon_fa, lon_fb, lon_ba, lon_bb, in_a, in_b, mix_hi, mix_lo, fin_f, fin_b, ent_f, ent_b,
    lat_f, lat_b, minc, weighted, red_a, red_c, tile,
    in_sem, out_sem, lon_s, lon_r, lat_s, lat_r, mem_s, mem_r, ra_s, ra_r, rc_s, rc_r,
):
    me_lon, me_lat, me_mem = lax.axis_index("lon"), lax.axis_index("lat"), lax.axis_index("mem")

    barrier = pltpu.get_barrier_semaphore()
    for axis, me, count in (("lon", me_lon, LON), ("lat", me_lat, LAT), ("mem", me_mem, MEM)):
        for delta in (1, LAT - 1) if axis == "lat" else far_first(count):
            pl.semaphore_signal(
                barrier, inc=1, device_id={axis: lax.rem(me + delta, count)}, device_id_type=MESH
            )

    load_d = pltpu.make_async_copy(direction, dvm, in_sem.at[0])
    load_m = pltpu.make_async_copy(members, mvm, in_sem.at[1])
    load_o = pltpu.make_async_copy(obs_weight, ovm, in_sem.at[2])
    load_r = pltpu.make_async_copy(residual, rvm, in_sem.at[3])
    small = [
        pltpu.make_async_copy(lon_decay_in, lon_decay, in_sem.at[4]),
        pltpu.make_async_copy(lat_decay_in, lat_decay, in_sem.at[5]),
        pltpu.make_async_copy(vert_modes_in, vert_modes, in_sem.at[6]),
        pltpu.make_async_copy(eig_count_in, eig_count, in_sem.at[7]),
    ]
    for load in (*small, load_d, load_m, load_o, load_r):
        load.start()
    for load in small:
        load.wait()

    row, c_row = row_values((STATES, COLS), lon_decay)
    section = row % 4
    column = iota((STATES, COLS), 1).astype(F32)

    def pick(entries):
        result = entries[3]
        for s in range(3):
            result = jnp.where(section == s, entries[s], result)
        return result

    gain_row = lon_gain(c_row)
    last = COLS - 1.0
    fin_f[...] = pick([rising(last - column, s) for s in range(4)]) * jnp.exp(-(last - column) * c_row)
    fin_b[...] = pick([rising(column, s) for s in range(4)]) * jnp.exp(-column * c_row)
    ent_f[...] = (
        gain_row * pick([rising(column, 3 - s) for s in range(4)]) * jnp.exp(-(column + 1.0) * c_row)
    )
    ent_b[...] = (
        gain_row
        * pick([rising(last - column, 3 - s) for s in range(4)])
        * jnp.exp(-(last - column + 1.0) * c_row)
    )

    source = iota((COLS, COLS), 0)
    target = iota((COLS, COLS), 1)

    def response(offset, y):
        lag = jnp.maximum(offset, 0).astype(F32)
        c = jnp.full((COLS, COLS), lon_decay[y], F32)
        gain = lon_gain(jnp.full((8, COLS), lon_decay[y], F32))[0:1]
        return jnp.where(offset >= 0, rising(lag, 3) * gain * jnp.exp(-lag * c), 0.0)

    def tables_f(y, carry):
        kf_hi[y], kf_lo[y] = halves(response(target - source, y))
        return carry

    def tables_b(y, carry):
        kb_hi[y], kb_lo[y] = halves(response(source - target, y))
        return carry

    lax.fori_loop(0, ROWS, tables_f, 0)

    c_lat = lat_decay[...]
    q = jnp.broadcast_to(jnp.exp(-c_lat), (CHUNK, COLS))
    a_lat = leak(c_lat)
    gain_lat = jnp.broadcast_to(a_lat * a_lat * a_lat * jnp.sqrt(a_lat) * 2.5, (CHUNK, COLS))

    lon_slots = ((lon_fa, lon_fb), (lon_ba, lon_bb))
    lon_in = (in_a, in_b)

    def lon_states(get_plane, fin, phase, g):
        first, count = GROUPS[g]
        total = jnp.zeros((STATES, count), F32)
        for y in range(ROWS):
            weights = jnp.where(row // 4 == y, fin[...], 0.0)
            total = total + dot3(halves(weights), halves(get_plane(y, first, count)), ((1,), (1,)))
        lon_slots[phase][g][pl.ds((LON - 1) * STATES, STATES), :] = total

    def lon_copy(phase, g, delta):
        sign = 1 if phase == 0 else LON - 1
        slots = lon_slots[phase][g]
        return pltpu.make_async_remote_copy(
            src_ref=slots.at[pl.ds((LON - 1) * STATES, STATES)],
            dst_ref=slots.at[pl.ds((delta - 1) * STATES, STATES)],
            send_sem=lon_s.at[phase, g, delta - 1],
            recv_sem=lon_r.at[phase, g, delta - 1],
            device_id={"lon": lax.rem(me_lon + sign * delta, LON)},
            device_id_type=MESH,
        )

    def lon_mix():
        shape = (STATES, LON * STATES)
        to_row, c = row_values(shape, lon_decay)
        from_col = iota(shape, 1)
        same = (from_col % STATES) // 4 == to_row // 4
        spread = to_row % 4 - from_col % 4
        cells = ((from_col // STATES) * COLS).astype(F32)
        closing = jnp.exp(-cells * c)
        t = [closing * rising(cells - 1.0, k) for k in range(4)]
        circle = jnp.full(shape, float(COLS * LON), F32)
        closed = jnp.exp(-circle * c)
        n = [closed * rising(circle - 1.0, k) for k in range(4)]
        p = [1.0 / (1.0 - n[0])]
        p.append(p[0] * (n[1] * p[0]))
        p.append(p[0] * (n[1] * p[1] + n[2] * p[0]))
        p.append(p[0] * (n[1] * p[2] + n[2] * p[1] + n[3] * p[0]))
        m = [sum(t[j] * p[k - j] for j in range(k + 1)) for k in range(4)]
        mix = jnp.zeros(shape, F32)
        for k in range(4):
            mix = jnp.where(same & (spread == k), m[k], mix)
        mix_hi[...], mix_lo[...] = halves(mix)

    def lon_incoming(phase, g):
        for delta in range(1, LON):
            lon_copy(phase, g, delta).wait_recv()
        mix = (mix_hi[...], mix_lo[...])
        incoming = dot3(mix, halves(lon_slots[phase][g][...]), ((1,), (0,)))
        lon_in[g][...] = jnp.transpose(incoming)

    def enter(y, ent, g):
        weights = jnp.where(row // 4 == y, ent[...], 0.0)
        return dot3(halves(lon_in[g][...]), halves(weights), ((1,), (0,)))

    lon_mix()
    load_d.wait()

    def d_plane(y, first=0, count=FIELDS):
        return dvm[pl.ds(first * ROWS + y, count, stride=ROWS), :]

    lon_states(d_plane, fin_f, 0, 0)
    lon_states(d_plane, fin_f, 0, 1)
    pl.semaphore_wait(barrier, LON - 1 + 2 + MEM - 1)
    for g in range(2):
        for delta in far_first(LON):
            lon_copy(0, g, delta).start()

    def inside_f(y, carry):
        planes[y] = dot3(halves(d_plane(y)), (kf_hi[y], kf_lo[y]), ((1,), (0,)))
        return carry

    lax.fori_loop(0, ROWS, inside_f, 0)

    def entered_f(g):
        lon_incoming(0, g)
        at = pl.ds(*GROUPS[g])
        for y in range(ROWS):
            planes[y, at, :] = planes[y, at, :] + enter(y, ent_f, g)

    OWN, AHEAD_IN, TOTAL_IN, AHEAD_OUT, TOTAL_OUT = range(5)

    def lat_copy(bufs, phase, c, source, ahead, step):
        sign = step if phase == 0 else -step
        stream = 0 if ahead else 1
        return pltpu.make_async_remote_copy(
            src_ref=bufs.at[source, c],
            dst_ref=bufs.at[AHEAD_IN if ahead else TOTAL_IN, c],
            send_sem=lat_s.at[phase, stream, c],
            recv_sem=lat_r.at[phase, stream, c],
            device_id={"lat": lax.rem(me_lat + (LAT + sign), LAT)},
            device_id_type=MESH,
        )

    def advance(v, f):
        v1 = q * v[0] + f
        v2 = q * v[1] + v1
        v3 = q * v[2] + v2
        v4 = q * v[3] + v3
        return [v1, v2, v3, v4]

    def own_states(get_row, order, bufs, c):
        v = [jnp.zeros((CHUNK, COLS), F32)] * 4
        for y in order:
            v = advance(v, get_row(y))
        for s in range(4):
            bufs[OWN, c, s] = v[s]

    def transition(cells):
        closing = jnp.exp(-cells * c_lat)
        offset = jnp.zeros((1, COLS), F32) + (cells - 1.0)
        return [jnp.broadcast_to(closing * rising(offset, k), (CHUNK, COLS)) for k in range(4)]

    one_block = transition(float(ROWS))

    def add_moved(move, moved, fixed, result, bufs, c):
        v = [bufs[moved, c, s] for s in range(4)]
        w = [bufs[fixed, c, s] for s in range(4)]
        for s in range(4):
            total = w[s]
            for j in range(s + 1):
                total = total + move[s - j] * v[j]
            bufs[result, c, s] = total

    def is_in(p, *places):
        return functools.reduce(jnp.logical_or, [p == k for k in places])

    def places_of(phase):
        p = me_lat if phase == 0 else LAT - 1 - me_lat
        blocks = jnp.where(p < 4, 3 - p, p - 4)
        return p, transition((blocks * ROWS).astype(F32))

    def lat_begin(bufs, phase, p, c):
        @pl.when(is_in(p, 0, 4))
        def _():
            lat_copy(bufs, phase, c, OWN, True, 1).start()

        @pl.when(p == 3)
        def _():
            lat_copy(bufs, phase, c, OWN, False, -1).start()

        @pl.when(p == 0)
        def _():
            bufs[AHEAD_IN, c] = jnp.zeros((4, CHUNK, COLS), F32)

    def lat_streams(bufs, phase, p, far, prepare=None):
        wait_all = 0 if prepare is None else CHUNKS
        late_ahead = jnp.where(p == 2, LAG, jnp.where(p == 3, wait_all, 0))
        late_total = jnp.where(p == 1, LAG, jnp.where(p == 0, wait_all, 0))

        def chunk_of(t):
            return lax.rem(t + (FIRST if phase == 0 else 0) + CHUNKS, CHUNKS)

        def step(t, carry):
            a_at, b_at = t - late_ahead, t - late_total
            a, b = chunk_of(a_at), chunk_of(b_at)
            if prepare is not None:

                @pl.when((lax.rem(t, GROUP) == 0) & (t < CHUNKS))
                def _():
                    prepare(t // GROUP)


            @pl.when(is_in(p, 1, 2, 3, 5, 6) & (a_at >= 0) & (a_at < CHUNKS))
            def _():
                lat_copy(bufs, phase, a, AHEAD_OUT, True, 1).wait_recv()
                add_moved(one_block, AHEAD_IN, OWN, AHEAD_OUT, bufs, a)
                lat_copy(bufs, phase, a, AHEAD_OUT, True, 1).start()

            @pl.when((p < 3) & (b_at >= 0) & (b_at < CHUNKS))
            def _():
                lat_copy(bufs, phase, b, TOTAL_OUT, False, -1).wait_recv()
                add_moved(far, OWN, TOTAL_IN, TOTAL_OUT, bufs, b)
                lat_copy(bufs, phase, b, TOTAL_OUT, False, -1).start()

            return carry

        lax.fori_loop(0, CHUNKS + max(LAG, wait_all), step, 0)

    def lat_finish(bufs, phase, p, far, c):
        @pl.when(is_in(p, 4, 7))
        def _():
            lat_copy(bufs, phase, c, AHEAD_OUT, True, 1).wait_recv()

        @pl.when(p == 4)
        def _():
            lat_copy(bufs, phase, c, AHEAD_IN, False, 1).start()

        @pl.when(p > 4)
        def _():
            lat_copy(bufs, phase, c, TOTAL_OUT, False, -1).wait_recv()

        @pl.when(p == 7)
        def _():
            lat_copy(bufs, phase, c, TOTAL_IN, False, -1).start()

        @pl.when(p > 4)
        def _():
            add_moved(far, TOTAL_IN, AHEAD_IN, AHEAD_IN, bufs, c)

        return [bufs[AHEAD_IN, c, s] for s in range(4)]

    def lat_left(bufs, phase, p):
        def left(c, carry):
            @pl.when(p < 7)
            def _():
                lat_copy(bufs, phase, c, AHEAD_OUT, True, 1).wait_send()

            @pl.when((p < 5) | (p == 7))
            def _():
                lat_copy(bufs, phase, c, TOTAL_OUT, False, -1).wait_send()

            return carry

        lax.fori_loop(0, CHUNKS, left, 0)

    p_f, far_f = places_of(0)
    p_b, far_b = places_of(1)

    def fields_of(c):
        return pl.ds(pl.multiple_of(c * CHUNK, CHUNK), CHUNK)

    def start_f(c, carry):
        own_states(lambda y: planes[y, fields_of(c), :], range(ROWS), lat_f, c)
        lat_begin(lat_f, 0, p_f, c)
        return carry

    entered_f(0)
    lax.fori_loop(FIRST, CHUNKS, start_f, 0)
    entered_f(1)
    lax.fori_loop(0, FIRST, start_f, 0)

    for e in range(MODES):
        for l in range(LEVELS):
            vtab[l * MODES + e] = jnp.full((8, COLS), vert_modes[e, l], F32)
    lax.fori_loop(0, ROWS, tables_b, 0)
    load_m.wait()
    minc[me_mem] = jnp.zeros((LEVELS * ROWS, COLS), F32)

    mode = iota((CHUNK, COLS), 0)

    def active(c):
        return jnp.where(mode < eig_count[c], 1.0, 0.0)

    lat_streams(lat_f, 0, p_f, far_f)

    def chain_f(turn, carry):
        g = lax.rem(turn + FIRST // GROUP, CHUNKS // GROUP)
        w = []
        for k in range(GROUP):
            c = g * GROUP + k
            v = lat_finish(lat_f, 0, p_f, far_f, c)
            scale = gain_lat * active(c)
            for y in range(ROWS):
                v = advance(v, planes[y, fields_of(c), :])
                nat[pl.ds(c * (CHUNK * ROWS) + y, CHUNK, stride=ROWS), :] = v[3] * scale
            base = pl.multiple_of(c * (CHUNK * ROWS), CHUNK * ROWS)
            w.append([nat[pl.ds(base + e * ROWS, ROWS), :] for e in range(MODES)])

        def levels(pair, carry):
            at = pl.ds(pl.multiple_of(pair * 16, 16), 16)
            ens = [mvm[g * GROUP + m, at, :].astype(F32) for m in range(GROUP)]
            for h in range(2):
                total = None
                for m in range(GROUP):
                    profile = None
                    for e in range(MODES):
                        term = vtab[(pair * 2 + h) * MODES + e] * w[m][e]
                        profile = term if profile is None else profile + term
                    term = ens[m][h * 8 : h * 8 + 8] * profile
                    total = term if total is None else total + term
                at = pl.ds(pl.multiple_of(pair * 16 + h * 8, 8), 8)
                minc[me_mem, at, :] = minc[me_mem, at, :] + total
            return carry

        lax.fori_loop(0, LEVELS // 2, levels, 0)
        return carry

    lax.fori_loop(0, CHUNKS // GROUP, chain_f, 0)

    def mem_copy(delta):
        return pltpu.make_async_remote_copy(
            src_ref=minc.at[me_mem],
            dst_ref=minc.at[me_mem],
            send_sem=mem_s.at[delta - 1],
            recv_sem=mem_r.at[delta - 1],
            device_id={"mem": lax.rem(me_mem + delta, MEM)},
            device_id_type=MESH,
        )

    for delta in far_first(MEM):
        mem_copy(delta).start()
    load_o.wait()
    for delta in range(1, MEM):
        mem_copy(delta).wait_recv()
    weighted[...] = ovm[...] * ((minc[0] + minc[1]) + (minc[2] + minc[3]))

    def start_b(g):
        def levels(pair, total):
            total = list(total)
            at = pl.ds(pl.multiple_of(pair * 16, 16), 16)
            weight = weighted[at, :]
            for m in range(GROUP):
                both = mvm[g * GROUP + m, at, :].astype(F32) * weight
                for h in range(2):
                    for e in range(MODES):
                        total[m * MODES + e] = (
                            total[m * MODES + e]
                            + vtab[(pair * 2 + h) * MODES + e] * both[h * 8 : h * 8 + 8]
                        )
            return tuple(total)

        zero = jnp.zeros((8, COLS), F32)
        total = lax.fori_loop(0, LEVELS // 2, levels, (zero,) * (GROUP * MODES))
        for k in range(GROUP):
            c = g * GROUP + k
            base = pl.multiple_of(c * (CHUNK * ROWS), CHUNK * ROWS)
            for e in range(MODES):
                nat[pl.ds(base + e * ROWS, ROWS), :] = total[k * MODES + e]
            mask = active(c)
            for y in range(ROWS):
                planes[y, fields_of(c), :] = (
                    nat[pl.ds(c * (CHUNK * ROWS) + y, CHUNK, stride=ROWS), :] * mask
                )
            own_states(lambda y: planes[y, fields_of(c), :], range(ROWS - 1, -1, -1), lat_b, c)
            lat_begin(lat_b, 1, p_b, c)

    lat_streams(lat_b, 1, p_b, far_b, start_b)

    def chain_b(c, carry):
        v = lat_finish(lat_b, 1, p_b, far_b, c)
        for y in range(ROWS - 1, -1, -1):
            v = advance(v, planes[y, fields_of(c), :])
            planes[y, fields_of(c), :] = v[3] * gain_lat
        return carry

    def z_plane(y, first, count):
        return planes[y, pl.ds(first, count), :]

    lax.fori_loop(0, FIRST, chain_b, 0)
    lon_states(z_plane, fin_b, 1, 1)
    for delta in far_first(LON):
        lon_copy(1, 1, delta).start()
    lax.fori_loop(FIRST, CHUNKS, chain_b, 0)
    lon_states(z_plane, fin_b, 1, 0)
    for delta in far_first(LON):
        lon_copy(1, 0, delta).start()

    def inside_b(y, carry):
        planes[y] = dot3(halves(planes[y]), (kb_hi[y], kb_lo[y]), ((1,), (0,)))
        return carry

    lax.fori_loop(0, ROWS, inside_b, 0)
    load_r.wait()
    sums = [jnp.zeros((8, COLS), F32)] * 4
    stores = []
    for g in (1, 0):
        first, count = GROUPS[g]
        lon_incoming(1, g)
        for y in range(ROWS):
            at = pl.ds(first * ROWS + y, count, stride=ROWS)
            d, r = dvm[at, :], rvm[at, :]
            h = d + (z_plane(y, first, count) + enter(y, ent_b, g))
            nat[at, :] = h
            for k, product in enumerate((r * r, d * h, r * h, h * h)):
                sums[k] = sums[k] + jnp.sum(product.reshape(count // 8, 8, COLS), axis=0)
        part = pl.ds(first * ROWS, count * ROWS)
        stores.append(pltpu.make_async_copy(nat.at[part], hess_out.at[part], out_sem.at[g]))
        stores[-1].start()

    for k in range(4):
        tile[pl.ds(k, 1), :] = jnp.sum(sums[k], axis=0, keepdims=True)
    tile[pl.ds(4, 4), :] = jnp.zeros((4, COLS), F32)

    def reduce(slots, me, s_sem, r_sem, peers, meanwhile):
        slots[me] = tile[...]

        def copies():
            for k, peer in enumerate(peers):
                yield pltpu.make_async_remote_copy(
                    src_ref=slots.at[me],
                    dst_ref=slots.at[me],
                    send_sem=s_sem.at[k],
                    recv_sem=r_sem.at[k],
                    device_id=peer,
                    device_id_type=MESH,
                )

        for copy in copies():
            copy.start()
        meanwhile()
        for copy in copies():
            copy.wait_recv()
        total = slots[0]
        for k in range(1, len(peers) + 1):
            total = total + slots[k]
        tile[...] = total
        return copies

    def departed():
        for store in stores:
            store.wait()
        for phase in range(2):
            for g in range(2):
                for delta in range(1, LON):
                    lon_copy(phase, g, delta).wait_send()
        for delta in range(1, MEM):
            mem_copy(delta).wait_send()
        lat_left(lat_f, 0, p_f)
        lat_left(lat_b, 1, p_b)

    def departed_a():
        for copy in left_a():
            copy.wait_send()

    left_a = reduce(
        red_a, me_mem * LON + me_lon, ra_s, ra_r,
        [
            {"lon": lax.rem(me_lon + dx, LON), "mem": lax.rem(me_mem + dy, MEM)}
            for dx, dy in sorted(
                [(dx, dy) for dy in range(MEM) for dx in range(LON) if dx or dy],
                key=lambda d: -(min(d[1], MEM - d[1]) + min(d[0], LON - d[0]) / 2),
            )
        ],
        departed,
    )
    left_c = reduce(
        red_c, me_lat, rc_s, rc_r, [{"lat": lax.rem(me_lat + dz, LAT)} for dz in far_first(LAT)],
        departed_a,
    )
    sums = jnp.broadcast_to(jnp.sum(tile[...], axis=1, keepdims=True), (8, COLS))
    rr, dh, rh, hh = (sums[k : k + 1] for k in range(4))
    step = rr / dh
    norm_new = rr - 2.0 * step * rh + step * step * hh
    step_out[0, 0] = step[0, 0]
    ratio_out[0, 0] = (norm_new / rr)[0, 0]

    for copy in left_c():
        copy.wait_send()


def body(control, residual, direction, members, vert_modes, eig_count, lon_decay, lat_decay, obs_weight):
    rows = FIELDS * ROWS
    any_space = pl.BlockSpec(memory_space=pl.ANY)
    smem = pl.BlockSpec(memory_space=pltpu.SMEM)
    dma = pltpu.SemaphoreType.DMA
    states = pltpu.VMEM((5, CHUNKS, 4, CHUNK, COLS), F32)
    table = pltpu.VMEM((ROWS, COLS, COLS), BF16)
    slots = [pltpu.VMEM((LON * STATES, count), F32) for first, count in GROUPS]
    mix = pltpu.VMEM((STATES, LON * STATES), BF16)
    small = pltpu.VMEM((STATES, COLS), F32)
    one = jax.ShapeDtypeStruct((1, 1), F32)
    hessian, step, ratio = pl.pallas_call(
        kernel,
        name="cg_step",
        out_shape=(
            jax.ShapeDtypeStruct((rows, COLS), F32),
            one, one,
        ),
        in_specs=[any_space] * 8,
        out_specs=(any_space, smem, smem),
        scratch_shapes=[
            pltpu.SMEM(vert_modes.shape, F32),
            pltpu.SMEM(eig_count.shape, jnp.int32),
            pltpu.SMEM(lon_decay.shape, F32),
            pltpu.VMEM((1, COLS), F32),
            pltpu.VMEM((rows, COLS), F32),
            pltpu.VMEM((rows, COLS), F32),
            pltpu.VMEM((FIELDS // MODES, LEVELS * ROWS, COLS), BF16),
            pltpu.VMEM((LEVELS * ROWS, COLS), F32),
            pltpu.VMEM((rows, COLS), F32),
            pltpu.VMEM((ROWS, FIELDS, COLS), F32),
            table, table, table, table,
            pltpu.VMEM((LEVELS * MODES, 8, COLS), F32),
            *slots, *slots,
            *[pltpu.VMEM((count, STATES), F32) for first, count in GROUPS],
            mix, mix,
            small, small, small, small,
            states, states,
            pltpu.VMEM((MEM, LEVELS * ROWS, COLS), F32),
            pltpu.VMEM((LEVELS * ROWS, COLS), F32),
            pltpu.VMEM((LON * MEM, 8, COLS), F32),
            pltpu.VMEM((LAT, 8, COLS), F32),
            pltpu.VMEM((8, COLS), F32),
            dma((8,)), dma((2,)),
            dma((2, 2, LON - 1)), dma((2, 2, LON - 1)),
            dma((2, 2, CHUNKS)), dma((2, 2, CHUNKS)),
            dma((MEM - 1,)), dma((MEM - 1,)),
            dma((LON * MEM - 1,)), dma((LON * MEM - 1,)),
            dma((LAT - 1,)), dma((LAT - 1,)),
        ],
        compiler_params=pltpu.CompilerParams(
            collective_id=0, has_side_effects=True, vmem_limit_bytes=60 << 20
        ),
    )(
        direction.reshape(rows, COLS),
        residual.reshape(rows, COLS),
        members.reshape(FIELDS // MODES, LEVELS * ROWS, COLS),
        vert_modes,
        eig_count,
        lon_decay,
        lat_decay.reshape(1, COLS),
        obs_weight.reshape(LEVELS * ROWS, COLS),
    )
    hessian = hessian.reshape(direction.shape)
    step, ratio = step.reshape(()), ratio.reshape(())
    new_control = control + step * direction
    new_residual = residual - step * hessian
    new_direction = new_residual + ratio * direction
    return new_control, new_residual, new_direction


def solution(mesh):
    field = P("mem", "lat", "lon")
    placed = (
        field, field, field, P("mem", None, "lat", "lon"), P(), P("mem"), P("lat"), P("lon"),
        P(None, "lat", "lon"),
    )
    return jax.shard_map(
        body, mesh=mesh, in_specs=placed, out_specs=(field, field, field), check_vma=False
    )
```
